32 devices in a mesh: grp: 2 (over y), wa: 4 (over z), col: 2 (over x), row: 2 (over core).
Axes of the slice: x: 2, y: 2, z: 4, core: 2. Of those that a mesh axis runs over, the one named last changes fastest.
Arguments:
- walkers: bfloat16 [64, 1024, 384], P(('grp', 'wa', 'col', 'row')), parts along dimension 0, may hold values from -2 to 2
- intersection_inverse: bfloat16 [64, 384, 384], P(('grp', 'wa', 'col', 'row')), parts along dimension 0, may hold values from -0.3125 to 0.3125
- noise_index: int32 [64, 64], P(('grp', 'wa', 'col', 'row')), parts along dimension 0, may hold values from 0 to 65535
- cholesky: bfloat16 [64, 1024, 1024], P(None, ('wa', 'col')), may hold values from -0.21875 to 0.21875
Outputs:
- walkers_new: bfloat16 [64, 1024, 384], P(('grp', 'wa', 'col', 'row')), parts along dimension 0
- log_weight: float32 [64], P(('grp', 'wa', 'col', 'row')), parts along dimension 0
The draws below stay inside these ranges and needn't reach their ends.
There are 2 independent parts, one for each index of `grp`. The reference program is written for one: setup_inputs(seed, part) draws one part's arguments, and reference() takes and returns one part's arrays. A program takes and returns all parts, laid end to end along the dimension named above; an argument that names none is the same for every part. Nothing has to cross between parts.
All inputs are finite; a program needn't handle non-finite values.
Results may differ from the reference program's by a relative error of at most 0.006.
Values may be sent and summed in bfloat16 or wider, within the bound.
No kernel may reach another device: no remote copies, remote signals or barrier semaphores. Data moves between devices by JAX's collectives and lax.ppermute only.
A program may use at most 128 MiB of HBM per device.

```python
import jax
import jax.numpy as jnp
from jax import lax

N = 1024
NE = 384
NCHOL = 64
NOISE_LEVELS = 65536
W = 32


def place_ends(array, rng, least, top_value):
    index_at = [jax.random.randint(jax.random.fold_in(rng, axis), (), 0, length) for axis, length in enumerate(array.shape)]
    widest = array.shape.index(max(array.shape))
    neighbour = index_at[:widest] + [(index_at[widest] + 1) % array.shape[widest]] + index_at[widest + 1:]
    return array.at[tuple(index_at)].set(least).at[tuple(neighbour)].set(top_value)


def block_levels(rng, dims, shards, least, largest):
    def one(position, shards_of):
        steps = jax.random.uniform(jax.random.fold_in(jax.random.fold_in(rng, 6), position), (shards_of,), jnp.float32, least / len(shards), largest / len(shards))
        return jnp.repeat(jnp.exp(steps), dims[position] // shards_of).reshape((-1,) + (1,) * (len(dims) - position - 1))

    level = one(*shards[0])
    for cut in shards[1:]:
        level = level * one(*cut)
    return level


def centred(own_key, shape, spread, limit, split=(), kind=jnp.bfloat16):
    values = spread * jax.random.normal(own_key, shape, jnp.float32)
    if split:
        values = values * block_levels(own_key, shape, split, -0.22, 0.18)
    return jnp.clip(values, -limit, limit).astype(kind)


def setup_inputs(seed: int = 0, part: int = 0) -> dict:
    key_list = jax.random.split(jax.random.key(seed), 5)
    part_keys = jax.random.split(jax.random.fold_in(key_list[4], part), 5)
    return {
        "walkers": centred(part_keys[0], (W, N, NE), 0.35, 2.0, ((0, 16),)),
        "intersection_inverse": centred(part_keys[1], (W, NE, NE), NE ** -0.5, 0.3125, ((0, 16),)),
        "noise_index": place_ends(jax.random.randint(part_keys[2], (W, NCHOL), 0, NOISE_LEVELS), jax.random.fold_in(part_keys[2], 1), 0, NOISE_LEVELS - 1).astype(jnp.int32),
        "cholesky": centred(key_list[3], (NCHOL, N, N), (12 * NCHOL) ** -0.5, 0.21875, ((1, 8),)),
    }


STEP_ROOT = 0.1
BIAS_CAP = 1.0
ROOT_TWO = 1.4142135623730951


def normal_quantile(code_row):
    level = (code_row.astype(jnp.float32) + 0.5) / NOISE_LEVELS
    return ROOT_TWO * lax.erf_inv(2.0 * level - 1.0)


def reference(walkers, intersection_inverse, noise_index, cholesky):
    half_rows = cholesky[:, :, :NE].reshape(NCHOL, N * NE)
    full_rows = cholesky.reshape(NCHOL, N * N)

    def advance(packed):
        walker_mat, inverse_mat, code_row = packed
        green_half = jnp.dot(walker_mat, inverse_mat, preferred_element_type=jnp.float32).astype(jnp.bfloat16)
        bias_sum = jnp.dot(half_rows, green_half.reshape(N * NE), preferred_element_type=jnp.float32)
        force_bias = jnp.clip(STEP_ROOT * bias_sum, -BIAS_CAP, BIAS_CAP)
        noise = normal_quantile(code_row)
        shifted = noise - force_bias
        log_step = jnp.sum(shifted * force_bias - 0.5 * force_bias * force_bias)
        field = shifted.astype(jnp.bfloat16)
        potential = jnp.dot(field, full_rows, preferred_element_type=jnp.float32).astype(jnp.bfloat16).reshape(N, N)
        running = walker_mat.astype(jnp.float32)
        factor_term = walker_mat
        for degree in range(1, 5):
            product = (-STEP_ROOT / degree) * jnp.dot(potential, factor_term, preferred_element_type=jnp.float32)
            running = running + product
            factor_term = product.astype(jnp.bfloat16)
        return running.astype(jnp.bfloat16), log_step

    walkers_new, log_weight = lax.map(advance, (walkers, intersection_inverse, noise_index))
    return walkers_new, log_weight
```

```python
import functools

import jax
import jax.numpy as jnp
from jax import lax
from jax.experimental import pallas as pl
from jax.experimental.pallas import tpu as pltpu
from jax.sharding import PartitionSpec as P

NOISE_LEVELS = 65536


STEP_ROOT = 0.1
BIAS_CAP = 1.0
ROOT_TWO = 1.4142135623730951
DEGREES = 4
PLANE = ("wa", "col")
ROWS = 16
VMEM = 48 * 1024 * 1024


def bias_kernel(chol_ref, green_ref, out_ref, acc_ref):
    step = pl.program_id(0)
    vectors, rows, electrons = chol_ref.shape
    count = green_ref.shape[0]
    pairs = lax.dot_general(
        chol_ref[...].reshape(vectors * rows, electrons),
        green_ref[...].reshape(count * rows, electrons),
        (((1,), (1,)), ((), ())),
        preferred_element_type=jnp.float32,
    )

    @pl.when(step == 0)
    def _():
        acc_ref[...] = pairs

    @pl.when(step > 0)
    def _():
        acc_ref[...] += pairs

    @pl.when(step == pl.num_programs(0) - 1)
    def _():
        total = acc_ref[...].reshape(vectors, rows, count * rows)
        own = lax.broadcasted_iota(jnp.int32, total.shape, 1)
        other = lax.broadcasted_iota(jnp.int32, total.shape, 2) % rows
        summed = jnp.sum(jnp.where(own == other, total, 0.0), axis=1)
        fold_at = lax.broadcasted_iota(jnp.int32, (count, count * rows), 1) // rows
        fold = (fold_at == lax.broadcasted_iota(jnp.int32, (count, count * rows), 0)).astype(jnp.float32)
        out_ref[...] = lax.dot_general(
            fold,
            summed,
            (((1,), (1,)), ((), ())),
            preferred_element_type=jnp.float32,
            precision=lax.Precision.HIGHEST,
        )


def partial_bias(cholesky, green):
    vectors, tile_rows, _ = cholesky.shape
    count, _, electrons = green.shape
    if tile_rows % ROWS:
        return jnp.einsum("gpe,kpe->kg", cholesky[:, :, :electrons], green, preferred_element_type=jnp.float32)
    return pl.pallas_call(
        bias_kernel,
        grid=(tile_rows // ROWS,),
        in_specs=[
            pl.BlockSpec((vectors, ROWS, electrons), lambda t: (0, t, 0)),
            pl.BlockSpec((count, ROWS, electrons), lambda t: (0, t, 0)),
        ],
        out_specs=pl.BlockSpec((count, vectors), lambda t: (0, 0)),
        out_shape=jax.ShapeDtypeStruct((count, vectors), jnp.float32),
        scratch_shapes=[pltpu.VMEM((vectors * ROWS, count * ROWS), jnp.float32)],
        compiler_params=pltpu.CompilerParams(vmem_limit_bytes=VMEM),
        cost_estimate=pl.CostEstimate(
            flops=2 * vectors * ROWS * count * tile_rows * electrons,
            bytes_accessed=2 * (vectors + count) * tile_rows * electrons,
            transcendentals=0,
        ),
        name="bias_sum",
    )(cholesky, green)


def shifted_field(sums, noise):
    force_bias = jnp.clip(STEP_ROOT * jnp.sum(sums, axis=0), -BIAS_CAP, BIAS_CAP)
    return noise - force_bias, force_bias


def potential_kernel(sums_ref, noise_ref, chol_ref, out_ref, spread_ref):
    vectors, rows, orbitals = chol_ref.shape
    count = noise_ref.shape[0]

    @pl.when(pl.program_id(0) == 0)
    def _():
        shifted, _ = shifted_field(sums_ref[...], noise_ref[...])
        field = shifted.astype(jnp.bfloat16)
        widen_at = lax.broadcasted_iota(jnp.int32, (vectors, vectors * rows), 1) // rows
        widen = (widen_at == lax.broadcasted_iota(jnp.int32, (vectors, vectors * rows), 0)).astype(jnp.bfloat16)
        wide = jnp.dot(field, widen, preferred_element_type=jnp.float32)
        shape = (count, rows, vectors * rows)
        own = lax.broadcasted_iota(jnp.int32, shape, 1)
        other = lax.broadcasted_iota(jnp.int32, shape, 2) % rows
        spread = jnp.where(own == other, wide[:, None, :], 0.0)
        spread_ref[...] = spread.reshape(count * rows, vectors * rows).astype(jnp.bfloat16)

    out_ref[...] = (
        jnp.dot(
            spread_ref[...],
            chol_ref[...].reshape(vectors * rows, orbitals),
            preferred_element_type=jnp.float32,
        )
        .astype(jnp.bfloat16)
        .reshape(count, rows, orbitals)
    )


def potential_rows(sums, noise, cholesky):
    vectors, tile_rows, orbitals = cholesky.shape
    count = noise.shape[0]
    if tile_rows % ROWS:
        shifted, _ = shifted_field(sums, noise)
        return jnp.einsum(
            "kg,gpq->kpq", shifted.astype(jnp.bfloat16), cholesky, preferred_element_type=jnp.float32
        ).astype(jnp.bfloat16)
    return pl.pallas_call(
        potential_kernel,
        grid=(tile_rows // ROWS,),
        in_specs=[
            pl.BlockSpec(sums.shape, lambda t: (0, 0, 0)),
            pl.BlockSpec(noise.shape, lambda t: (0, 0)),
            pl.BlockSpec((vectors, ROWS, orbitals), lambda t: (0, t, 0)),
        ],
        out_specs=pl.BlockSpec((count, ROWS, orbitals), lambda t: (0, t, 0)),
        out_shape=jax.ShapeDtypeStruct((count, tile_rows, orbitals), jnp.bfloat16),
        scratch_shapes=[pltpu.VMEM((count * ROWS, vectors * ROWS), jnp.bfloat16)],
        compiler_params=pltpu.CompilerParams(vmem_limit_bytes=VMEM),
        cost_estimate=pl.CostEstimate(
            flops=2 * count * ROWS * vectors * tile_rows * orbitals,
            bytes_accessed=2 * (vectors + count) * tile_rows * orbitals,
            transcendentals=0,
        ),
        name="potential_rows",
    )(sums, noise, cholesky)


def taylor_kernel(potential_ref, walker_ref, out_ref):
    potential = potential_ref[...]
    term = walker_ref[...]
    running = term.astype(jnp.float32)
    for degree in range(1, DEGREES + 1):
        product = (-STEP_ROOT / degree) * jnp.dot(potential, term, preferred_element_type=jnp.float32)
        running = running + product
        term = product.astype(jnp.bfloat16)
    out_ref[...] = running.astype(jnp.bfloat16)


def taylor(potential, walker):
    orbitals, electrons = walker.shape
    return pl.pallas_call(
        taylor_kernel,
        out_shape=jax.ShapeDtypeStruct(walker.shape, jnp.bfloat16),
        compiler_params=pltpu.CompilerParams(vmem_limit_bytes=VMEM),
        cost_estimate=pl.CostEstimate(
            flops=2 * DEGREES * orbitals * orbitals * electrons,
            bytes_accessed=2 * orbitals * (orbitals + 2 * electrons),
            transcendentals=0,
        ),
        name="taylor",
    )(potential, walker)


def exchange(blocks):
    return lax.all_to_all(blocks, PLANE, 0, 0, tiled=True)


def gather(block):
    planes = lax.axis_size(PLANE)
    return exchange(jnp.broadcast_to(block[None], (planes,) + block.shape))


def per_device(walkers, intersection_inverse, noise_index, cholesky):
    walker_count, orbitals, electrons = walkers.shape
    vectors, tile_rows, _ = cholesky.shape
    planes = lax.axis_size(PLANE)
    me = lax.axis_index(PLANE)

    level = (noise_index.astype(jnp.float32) + 0.5) / NOISE_LEVELS
    noise = ROOT_TWO * lax.erf_inv(2.0 * level - 1.0)

    greens = []
    for k in range(walker_count):
        green = jnp.dot(walkers[k], intersection_inverse[k], preferred_element_type=jnp.float32)
        greens.append(exchange(green.astype(jnp.bfloat16).reshape(planes, tile_rows, electrons)))
    gathered = []
    for k in range(walker_count):
        sums = partial_bias(cholesky, greens[k])
        gathered.append(gather(jnp.concatenate([sums, noise[k : k + 1]], axis=0)))
    returned = []
    log_steps = []
    for k in range(walker_count):
        sums, noise_all = gathered[k][:, :planes], gathered[k][:, planes]
        returned.append(exchange(potential_rows(sums, noise_all, cholesky)))
        own_sums = lax.dynamic_index_in_dim(sums, me, 1, keepdims=False)
        shifted, force_bias = shifted_field(own_sums, noise[k])
        log_steps.append(jnp.sum(shifted * force_bias - 0.5 * force_bias * force_bias))
    new = [taylor(returned[k].reshape(orbitals, orbitals), walkers[k]) for k in range(walker_count)]
    return jnp.stack(new), jnp.stack(log_steps)


def solution(mesh):
    placed = (
        P(("grp", "wa", "col", "row"), None, None),
        P(("grp", "wa", "col", "row"), None, None),
        P(("grp", "wa", "col", "row"), None),
        P(None, ("wa", "col"), None),
    )
    return jax.shard_map(
        per_device,
        mesh=mesh,
        in_specs=placed,
        out_specs=(P(("grp", "wa", "col", "row"), None, None), P(("grp", "wa", "col", "row"))),
        check_vma=False,
    )
```

```python
import functools

import jax
import jax.numpy as jnp
from jax import lax
from jax.experimental import pallas as pl
from jax.experimental.pallas import tpu as pltpu
from jax.sharding import PartitionSpec as P

NOISE_LEVELS = 65536


STEP_ROOT = 0.1
BIAS_CAP = 1.0
ROOT_TWO = 1.4142135623730951
DEGREES = 4
PLANE = ("wa", "col")
ROWS = 16
MOST_PERMUTES = 8
VMEM = 24 * 1024 * 1024
IN_VMEM = pl.BlockSpec(memory_space=pltpu.VMEM)
IN_HBM = pl.BlockSpec(memory_space=pl.ANY)


def kernel_params():
    return pltpu.CompilerParams(vmem_limit_bytes=VMEM)


def quantile(codes):
    level = (codes.astype(jnp.float32) + 0.5) / NOISE_LEVELS
    return ROOT_TWO * lax.erf_inv(2.0 * level - 1.0)


def shifted_field(bias_sum, noise):
    force_bias = jnp.clip(STEP_ROOT * bias_sum, -BIAS_CAP, BIAS_CAP)
    shifted = noise - force_bias
    return shifted, shifted * force_bias - 0.5 * force_bias * force_bias


def iota(shape, dimension):
    return lax.broadcasted_iota(jnp.int32, shape, dimension)


def own_place():
    return lax.axis_index("wa") * lax.axis_size("col") + lax.axis_index("col")


def green_kernel(places, walker_ref, inverse_ref, *out_refs):
    me = own_place()
    inverse = inverse_ref[0]
    for place, out_ref in zip(places, out_refs):
        tile_rows = out_ref.shape[0]
        start = pl.multiple_of(jnp.bitwise_xor(me, place) * tile_rows, tile_rows)
        rows = walker_ref[0, pl.ds(start, tile_rows), :]
        out_ref[...] = jnp.dot(rows, inverse, preferred_element_type=jnp.float32).astype(jnp.bfloat16)


def green_rows(walkers, inverses, k, places, tile_rows):
    _, orbitals, electrons = walkers.shape
    return pl.pallas_call(
        functools.partial(green_kernel, places),
        grid=(1,),
        in_specs=[
            pl.BlockSpec((1, orbitals, electrons), lambda t: (k, 0, 0)),
            pl.BlockSpec((1, electrons, electrons), lambda t: (k, 0, 0)),
        ],
        out_specs=[pl.BlockSpec((tile_rows, electrons), lambda t: (0, 0))] * len(places),
        out_shape=[jax.ShapeDtypeStruct((tile_rows, electrons), jnp.bfloat16)] * len(places),
        compiler_params=kernel_params(),
        cost_estimate=pl.CostEstimate(
            flops=2 * len(places) * tile_rows * electrons * electrons,
            bytes_accessed=2 * electrons * (orbitals + electrons + len(places) * tile_rows),
            transcendentals=0,
        ),
        name="green_rows",
    )(walkers, inverses)


def bias_kernel(count, chol_ref, noise_ref, *refs):
    greens, out_ref = refs[:count], refs[count]
    vectors, tile_rows, _ = chol_ref.shape
    electrons = greens[0].shape[1]
    me = own_place()
    total = jnp.zeros((vectors * ROWS, count * ROWS), jnp.float32)
    for start in range(0, tile_rows, ROWS):
        green = jnp.concatenate([ref[start : start + ROWS, :] for ref in greens], axis=0)
        tile = chol_ref[:, start : start + ROWS, :electrons].reshape(vectors * ROWS, electrons)
        total += lax.dot_general(tile, green, (((1,), (1,)), ((), ())), preferred_element_type=jnp.float32)
    total = total.reshape(vectors, ROWS, count * ROWS)
    same = iota(total.shape, 1) == iota(total.shape, 2) % ROWS
    summed = jnp.sum(jnp.where(same, total, 0.0), axis=1)
    shape = (count, count * ROWS)
    fold = jnp.bitwise_xor(iota(shape, 1) // ROWS, me) == iota(shape, 0)
    out_ref[:count, :] = lax.dot_general(
        fold.astype(jnp.float32),
        summed,
        (((1,), (1,)), ((), ())),
        preferred_element_type=jnp.float32,
        precision=lax.Precision.HIGHEST,
    )
    out_ref[count:, :] = jnp.where(iota((count, vectors), 0) == me, noise_ref[...], 0.0)


def bias_rows(cholesky, noise, greens):
    vectors, tile_rows, _ = cholesky.shape
    count, electrons = len(greens), greens[0].shape[1]
    return pl.pallas_call(
        functools.partial(bias_kernel, count),
        in_specs=[IN_VMEM] * (2 + count),
        out_specs=IN_VMEM,
        out_shape=jax.ShapeDtypeStruct((2 * count, vectors), jnp.float32),
        compiler_params=kernel_params(),
        cost_estimate=pl.CostEstimate(
            flops=2 * vectors * ROWS * count * tile_rows * electrons,
            bytes_accessed=2 * (vectors + count) * tile_rows * electrons,
            transcendentals=0,
        ),
        name="bias_rows",
    )(pltpu.with_memory_space_constraint(cholesky, pltpu.VMEM), noise, *greens)


def potential_kernel(count, sums_ref, chol_ref, *refs):
    outs, log_ref = refs[:count], refs[count]
    vectors, tile_rows, orbitals = chol_ref.shape
    me = own_place()
    shifted, log_terms = shifted_field(sums_ref[:count, :], sums_ref[count:, :])
    log_ref[...] = jnp.sum(log_terms, axis=1, keepdims=True)
    field = shifted.astype(jnp.bfloat16)
    order = (jnp.bitwise_xor(iota((count, count), 0), me) == iota((count, count), 1)).astype(jnp.bfloat16)
    field = jnp.dot(order, field, preferred_element_type=jnp.float32).astype(jnp.bfloat16)
    widen = (iota((vectors, vectors * ROWS), 1) // ROWS == iota((vectors, vectors * ROWS), 0)).astype(jnp.bfloat16)
    wide = jnp.dot(field, widen, preferred_element_type=jnp.float32)
    shape = (count, ROWS, vectors * ROWS)
    spread = jnp.where(iota(shape, 1) == iota(shape, 2) % ROWS, wide[:, None, :], 0.0)
    spread = spread.reshape(count * ROWS, vectors * ROWS).astype(jnp.bfloat16)
    for start in range(0, tile_rows, ROWS):
        tile = chol_ref[:, start : start + ROWS, :].reshape(vectors * ROWS, orbitals)
        rows = jnp.dot(spread, tile, preferred_element_type=jnp.float32).astype(jnp.bfloat16)
        for place in range(count):
            outs[place][start : start + ROWS, :] = rows[place * ROWS : (place + 1) * ROWS, :]


def potential_rows(sums, cholesky):
    vectors, tile_rows, orbitals = cholesky.shape
    count = sums.shape[0] // 2
    rows = jax.ShapeDtypeStruct((tile_rows, orbitals), jnp.bfloat16)
    *blocks, log_steps = pl.pallas_call(
        functools.partial(potential_kernel, count),
        in_specs=[IN_VMEM, IN_VMEM],
        out_specs=[IN_VMEM] * (count + 1),
        out_shape=[rows] * count + [jax.ShapeDtypeStruct((count, 1), jnp.float32)],
        compiler_params=kernel_params(),
        cost_estimate=pl.CostEstimate(
            flops=2 * count * ROWS * vectors * tile_rows * orbitals,
            bytes_accessed=2 * (vectors + count) * tile_rows * orbitals,
            transcendentals=0,
        ),
        name="potential_rows",
    )(sums, pltpu.with_memory_space_constraint(cholesky, pltpu.VMEM))
    return blocks, log_steps


def taylor_steps(potential, term, product_of):
    running = term.astype(jnp.float32)
    for degree in range(1, DEGREES + 1):
        product = (-STEP_ROOT / degree) * product_of(potential, term)
        running = running + product
        term = product.astype(jnp.bfloat16)
    return running.astype(jnp.bfloat16)


def taylor_kernel(count, *refs):
    blocks, walker_ref, out_ref, held, arrived = refs[:count], *refs[count:]
    me = own_place()
    copies = [
        pltpu.make_async_copy(block, held.at[jnp.bitwise_xor(me, place)], arrived.at[place])
        for place, block in enumerate(blocks)
    ]
    for copy in copies:
        copy.start()
    for copy in copies:
        copy.wait()
    orbitals = held.shape[2]
    out_ref[0] = taylor_steps(
        held[...].reshape(orbitals, orbitals),
        walker_ref[0],
        lambda a, b: jnp.dot(a, b, preferred_element_type=jnp.float32),
    )


def taylor(blocks, walkers, k):
    _, orbitals, electrons = walkers.shape
    count, tile_rows = len(blocks), blocks[0].shape[0]
    return pl.pallas_call(
        functools.partial(taylor_kernel, count),
        grid=(1,),
        in_specs=[IN_HBM] * count + [pl.BlockSpec((1, orbitals, electrons), lambda t: (k, 0, 0))],
        out_specs=pl.BlockSpec((1, orbitals, electrons), lambda t: (0, 0, 0)),
        out_shape=jax.ShapeDtypeStruct((1, orbitals, electrons), jnp.bfloat16),
        scratch_shapes=[
            pltpu.VMEM((count, tile_rows, orbitals), jnp.bfloat16),
            pltpu.SemaphoreType.DMA((count,)),
        ],
        compiler_params=kernel_params(),
        cost_estimate=pl.CostEstimate(
            flops=2 * DEGREES * orbitals * orbitals * electrons,
            bytes_accessed=2 * orbitals * (orbitals + 2 * electrons),
            transcendentals=0,
        ),
        name="taylor",
    )(*blocks, walkers)


def swap(block, place):
    if place == 0:
        return block
    planes = lax.axis_size(PLANE)
    return lax.ppermute(block, PLANE, [(i, i ^ place) for i in range(planes)])


def by_permutes(walkers, intersection_inverse, noise_index, cholesky):
    walker_count = walkers.shape[0]
    tile_rows = cholesky.shape[1]
    planes = lax.axis_size(PLANE)
    far = tuple(range(planes // 2, planes))
    near = tuple(range(planes // 2))
    noise = quantile(noise_index)

    greens = []
    for k in range(walker_count):
        far_rows = green_rows(walkers, intersection_inverse, k, far, tile_rows)
        near_rows = green_rows(walkers, intersection_inverse, k, near, tile_rows)
        greens.append([swap(rows, place) for place, rows in enumerate((*near_rows, *far_rows))])
    sums = []
    for k in range(walker_count):
        total = bias_rows(cholesky, noise[k : k + 1], greens[k])
        distance = 1
        while distance < planes:
            total = total + swap(total, distance)
            distance *= 2
        sums.append(total)
    new, log_steps = [], []
    for k in range(walker_count):
        blocks, log_all = potential_rows(sums[k], cholesky)
        new.append(taylor([swap(rows, place) for place, rows in enumerate(blocks)], walkers, k))
        log_steps.append(lax.dynamic_index_in_dim(log_all[:, 0], lax.axis_index(PLANE), 0, keepdims=True))
    return jnp.concatenate(new, axis=0), jnp.concatenate(log_steps)


def by_all_to_all(walkers, intersection_inverse, noise_index, cholesky):
    walker_count, orbitals, electrons = walkers.shape
    vectors, tile_rows, _ = cholesky.shape
    planes = lax.axis_size(PLANE)
    green = jnp.einsum(
        "kpe,kef->kpf", walkers, intersection_inverse, preferred_element_type=jnp.float32
    ).astype(jnp.bfloat16)
    green = lax.all_to_all(
        green.reshape(walker_count, planes, tile_rows, electrons), PLANE, split_axis=1, concat_axis=1, tiled=True
    )
    partial_sums = jnp.einsum(
        "kspe,gpe->ksg", green, cholesky[:, :, :electrons], preferred_element_type=jnp.float32
    )
    bias_sum = lax.psum(partial_sums, PLANE)
    noise = lax.all_gather(quantile(noise_index), PLANE, axis=1, tiled=False)
    shifted, log_terms = shifted_field(bias_sum, noise)
    log_weight = lax.dynamic_index_in_dim(jnp.sum(log_terms, axis=-1), lax.axis_index(PLANE), 1, keepdims=False)
    rows = jnp.einsum(
        "ksg,gpq->kspq", shifted.astype(jnp.bfloat16), cholesky, preferred_element_type=jnp.float32
    ).astype(jnp.bfloat16)
    potential = lax.all_to_all(rows, PLANE, split_axis=1, concat_axis=1, tiled=True)
    new = taylor_steps(
        potential.reshape(walker_count, orbitals, orbitals),
        walkers,
        lambda a, b: jnp.einsum("kpq,kqe->kpe", a, b, preferred_element_type=jnp.float32),
    )
    return new, log_weight


def per_device(walkers, intersection_inverse, noise_index, cholesky):
    planes = lax.axis_size(PLANE)
    tile_rows = cholesky.shape[1]
    permutes = planes <= MOST_PERMUTES and planes & (planes - 1) == 0 and tile_rows % ROWS == 0
    step = by_permutes if permutes else by_all_to_all
    return step(walkers, intersection_inverse, noise_index, cholesky)


def solution(mesh):
    placed = (
        P(("grp", "wa", "col", "row"), None, None),
        P(("grp", "wa", "col", "row"), None, None),
        P(("grp", "wa", "col", "row"), None),
        P(None, ("wa", "col"), None),
    )
    return jax.shard_map(
        per_device,
        mesh=mesh,
        in_specs=placed,
        out_specs=(P(("grp", "wa", "col", "row"), None, None), P(("grp", "wa", "col", "row"))),
        check_vma=False,
    )
```

```python
import functools
import math

import jax
import jax.numpy as jnp
from jax import lax
from jax.experimental import pallas as pl
from jax.experimental.pallas import tpu as pltpu
from jax.sharding import PartitionSpec as P

NOISE_LEVELS = 65536


STEP_ROOT = 0.1
BIAS_CAP = 1.0
ROOT_TWO = 1.4142135623730951
DEGREES = 4
PLANE = ("wa", "col")
ROWS = 16
MOST_PERMUTES = 8
VMEM = 16 * 1024 * 1024
IN_VMEM = pl.BlockSpec(memory_space=pltpu.VMEM)
IN_HBM = pl.BlockSpec(memory_space=pltpu.HBM)
IN_ANY = pl.BlockSpec(memory_space=pl.ANY)


NO_COST = pl.CostEstimate(flops=0, bytes_accessed=0, transcendentals=0)


def kernel_params():
    return pltpu.CompilerParams(vmem_limit_bytes=VMEM)


def quantile(codes):
    level = (codes.astype(jnp.float32) + 0.5) / NOISE_LEVELS
    return ROOT_TWO * lax.erf_inv(2.0 * level - 1.0)


def shifted_field(bias_sum, noise):
    force_bias = jnp.clip(STEP_ROOT * bias_sum, -BIAS_CAP, BIAS_CAP)
    shifted = noise - force_bias
    return shifted, shifted * force_bias - 0.5 * force_bias * force_bias


def iota(shape, dimension):
    return lax.broadcasted_iota(jnp.int32, shape, dimension)


def own_place():
    return lax.axis_index("wa") * lax.axis_size("col") + lax.axis_index("col")


def in_hbm(array):
    return pltpu.with_memory_space_constraint(array, pltpu.HBM)


def device_at(place, relative):
    return jnp.bitwise_xor(own_place(), place) if relative else place


def green_kernel(k, groups, relative, walker_ref, inverse_ref, _, *refs):
    outs, (rows_in, inverse_in, arrived) = refs[: len(groups)], refs[len(groups) :]
    tile_rows = rows_in.shape[1]
    copies = [pltpu.make_async_copy(inverse_ref.at[k], inverse_in, arrived.at[0])]
    places = [place for place in sum(groups, ()) if place is not None]
    for i, place in enumerate(places):
        start = pl.multiple_of(device_at(place, relative) * tile_rows, tile_rows)
        copies.append(
            pltpu.make_async_copy(
                walker_ref.at[k, pl.ds(start, tile_rows), :], rows_in.at[i], arrived.at[i + 1]
            )
        )
    for copy in copies:
        copy.start()
    for copy in copies:
        copy.wait()
    rows = rows_in[...].reshape(-1, rows_in.shape[2])
    product = jnp.dot(rows, inverse_in[...], preferred_element_type=jnp.float32).astype(jnp.bfloat16)
    i = 0
    for group, out_ref in zip(groups, outs):
        for j, place in enumerate(group):
            if place is not None:
                out_ref[j] = product[i * tile_rows : (i + 1) * tile_rows, :]
                i += 1


def green_rows(walkers, inverses, k, tile_rows, groups, relative, after):
    _, orbitals, electrons = walkers.shape
    count = sum(place is not None for group in groups for place in group)
    return pl.pallas_call(
        functools.partial(green_kernel, k, groups, relative),
        in_specs=[IN_HBM, IN_HBM, IN_ANY],
        out_specs=[IN_VMEM] * len(groups),
        out_shape=[jax.ShapeDtypeStruct((len(group), tile_rows, electrons), jnp.bfloat16) for group in groups],
        scratch_shapes=[
            pltpu.VMEM((count, tile_rows, electrons), jnp.bfloat16),
            pltpu.VMEM((electrons, electrons), jnp.bfloat16),
            pltpu.SemaphoreType.DMA((count + 1,)),
        ],
        compiler_params=kernel_params(),
        cost_estimate=NO_COST,
        name="green_rows",
    )(in_hbm(walkers), in_hbm(inverses), after)


def load_kernel(chol_ref, _, held_ref, arrived):
    step = chol_ref.shape[0] // arrived.shape[0]
    copies = [
        pltpu.make_async_copy(chol_ref.at[pl.ds(i * step, step)], held_ref.at[pl.ds(i * step, step)], arrived.at[i])
        for i in range(arrived.shape[0])
    ]
    for copy in copies:
        copy.start()
    for copy in copies:
        copy.wait()


def load(cholesky, after):
    return pl.pallas_call(
        load_kernel,
        in_specs=[IN_HBM, IN_ANY],
        out_specs=IN_VMEM,
        out_shape=pltpu.VMEM(cholesky.shape, cholesky.dtype),
        scratch_shapes=[pltpu.SemaphoreType.DMA((math.gcd(cholesky.shape[0], 8),))],
        compiler_params=kernel_params(),
        cost_estimate=NO_COST,
        name="load_cholesky",
    )(in_hbm(cholesky), after)


def bias_kernel(where, relative, chol_ref, noise_ref, *refs):
    greens, out_ref = refs[:-1], refs[-1]
    count = len(where)
    vectors, tile_rows, _ = chol_ref.shape
    electrons = greens[0].shape[2]
    me = own_place()
    total = jnp.zeros((vectors * ROWS, count * ROWS), jnp.float32)
    for start in range(0, tile_rows, ROWS):
        green = jnp.concatenate([greens[i][j, start : start + ROWS, :] for i, j in where], axis=0)
        tile = chol_ref[:, start : start + ROWS, :electrons].reshape(vectors * ROWS, electrons)
        total += lax.dot_general(tile, green, (((1,), (1,)), ((), ())), preferred_element_type=jnp.float32)
    total = total.reshape(vectors, ROWS, count * ROWS)
    same = iota(total.shape, 1) == iota(total.shape, 2) % ROWS
    summed = jnp.sum(jnp.where(same, total, 0.0), axis=1)
    shape = (count, count * ROWS)
    source = iota(shape, 1) // ROWS
    fold = (jnp.bitwise_xor(source, me) if relative else source) == iota(shape, 0)
    out_ref[:count, :] = lax.dot_general(
        fold.astype(jnp.float32),
        summed,
        (((1,), (1,)), ((), ())),
        preferred_element_type=jnp.float32,
        precision=lax.Precision.HIGHEST,
    )
    out_ref[count:, :] = jnp.where(iota((count, vectors), 0) == me, noise_ref[...], 0.0)


def bias_rows(cholesky, noise, greens, where, relative):
    vectors, tile_rows, _ = cholesky.shape
    count, electrons = len(where), greens[0].shape[2]
    return pl.pallas_call(
        functools.partial(bias_kernel, where, relative),
        in_specs=[IN_VMEM] * (2 + len(greens)),
        out_specs=IN_VMEM,
        out_shape=jax.ShapeDtypeStruct((2 * count, vectors), jnp.float32),
        compiler_params=kernel_params(),
        cost_estimate=NO_COST,
        name="bias_rows",
    )(cholesky, noise, *greens)


def potential_kernel(groups, relative, parts, *refs):
    sums, chol_ref, outs, log_ref = refs[:parts], refs[parts], refs[parts + 2 : -1], refs[-1]
    places = [(place, out_ref, j) for group, out_ref in zip(groups, outs) for j, place in enumerate(group)]
    places = [slot for slot in places if slot[0] is not None]
    count = len(places)
    vectors, tile_rows, orbitals = chol_ref.shape
    totals = [ref[...] for ref in sums]
    total = totals[0] + sum(totals[2:], totals[1])
    shifted, log_terms = shifted_field(total[:count, :], total[count:, :])
    log_ref[...] = jnp.sum(log_terms, axis=1, keepdims=True)
    field = shifted.astype(jnp.bfloat16)
    if relative:
        order = jnp.bitwise_xor(iota((count, count), 0), own_place()) == iota((count, count), 1)
        field = jnp.dot(order.astype(jnp.bfloat16), field, preferred_element_type=jnp.float32).astype(jnp.bfloat16)
    widen = (iota((vectors, vectors * ROWS), 1) // ROWS == iota((vectors, vectors * ROWS), 0)).astype(jnp.bfloat16)
    wide = jnp.dot(field, widen, preferred_element_type=jnp.float32)
    shape = (count, ROWS, vectors * ROWS)
    spread = jnp.where(iota(shape, 1) == iota(shape, 2) % ROWS, wide[:, None, :], 0.0)
    spread = spread.reshape(count * ROWS, vectors * ROWS).astype(jnp.bfloat16)
    for start in range(0, tile_rows, ROWS):
        tile = chol_ref[:, start : start + ROWS, :].reshape(vectors * ROWS, orbitals)
        rows = jnp.dot(spread, tile, preferred_element_type=jnp.float32).astype(jnp.bfloat16)
        for place, out_ref, j in places:
            out_ref[j, start : start + ROWS, :] = rows[place * ROWS : (place + 1) * ROWS, :]


def potential_rows(sums, cholesky, groups, relative, after):
    vectors, tile_rows, orbitals = cholesky.shape
    count = sums[0].shape[0] // 2
    *blocks, log_steps = pl.pallas_call(
        functools.partial(potential_kernel, groups, relative, len(sums)),
        in_specs=[IN_VMEM] * (len(sums) + 1) + [IN_ANY],
        out_specs=[IN_VMEM] * (len(groups) + 1),
        out_shape=[
            *(jax.ShapeDtypeStruct((len(group), tile_rows, orbitals), jnp.bfloat16) for group in groups),
            jax.ShapeDtypeStruct((count, 1), jnp.float32),
        ],
        compiler_params=kernel_params(),
        cost_estimate=NO_COST,
        name="potential_rows",
    )(*sums, cholesky, after)
    return blocks, log_steps


def taylor_steps(potential, term, product_of):
    running = term.astype(jnp.float32)
    for degree in range(1, DEGREES + 1):
        product = (-STEP_ROOT / degree) * product_of(potential, term)
        running = running + product
        term = product.astype(jnp.bfloat16)
    return running.astype(jnp.bfloat16)


def taylor_kernel(k, where, relative, *refs):
    if relative:
        blocks, (walker_ref, _, _, out_ref, walker_in, result, arrived, held) = refs[:-8], refs[-8:]
    else:
        blocks, (walker_ref, _, _, out_ref, walker_in, result, arrived) = refs[:-7], refs[-7:]
        (held,) = blocks
    read = pltpu.make_async_copy(walker_ref.at[k], walker_in, arrived)
    read.start()
    if relative:
        for place, (i, j) in enumerate(where):
            held[device_at(place, relative)] = blocks[i][j]
    read.wait()
    orbitals = held.shape[2]
    result[...] = taylor_steps(
        held[...].reshape(orbitals, orbitals),
        walker_in[...],
        lambda a, b: jnp.dot(a, b, preferred_element_type=jnp.float32),
    )
    write = pltpu.make_async_copy(result, out_ref.at[k], arrived)
    write.start()
    write.wait()


def taylor(blocks, where, relative, walkers, k, new, after):
    _, orbitals, electrons = walkers.shape
    count, tile_rows = len(where), blocks[0].shape[1]
    held = [pltpu.VMEM((count, tile_rows, orbitals), jnp.bfloat16)] if relative else []
    return pl.pallas_call(
        functools.partial(taylor_kernel, k, where, relative),
        in_specs=[IN_VMEM] * len(blocks) + [IN_HBM, IN_HBM, IN_ANY],
        out_specs=IN_HBM,
        out_shape=jax.ShapeDtypeStruct(walkers.shape, jnp.bfloat16),
        scratch_shapes=[
            pltpu.VMEM((orbitals, electrons), jnp.bfloat16),
            pltpu.VMEM((orbitals, electrons), jnp.bfloat16),
            pltpu.SemaphoreType.DMA(()),
            *held,
        ],
        input_output_aliases={} if new is walkers else {len(blocks) + 1: 0},
        compiler_params=kernel_params(),
        cost_estimate=NO_COST,
        name="taylor",
    )(*blocks, in_hbm(walkers), in_hbm(new), after)


def swap(block, place):
    if place == 0:
        return block
    planes = lax.axis_size(PLANE)
    return lax.ppermute(block, PLANE, [(i, i ^ place) for i in range(planes)])


def join_kernel(moves, sources, *refs):
    outs, arrived = refs[-1 - (len(refs) - sources - 1) // 2 : -1], refs[-1]
    copies = [
        pltpu.make_async_copy(refs[i].at[pl.ds(j, 1)], outs[o].at[pl.ds(q, 1)], arrived.at[m])
        for m, ((i, j), (o, q)) in enumerate(moves)
    ]
    for copy in copies:
        copy.start()
    for copy in copies:
        copy.wait()


def join(sources, targets, moves):
    return pl.pallas_call(
        functools.partial(join_kernel, moves, len(sources)),
        in_specs=[IN_ANY] * (len(sources) + len(targets)),
        out_specs=[IN_ANY] * len(targets),
        out_shape=[jax.ShapeDtypeStruct(target.shape, target.dtype) for target in targets],
        input_output_aliases={len(sources) + i: i for i in range(len(targets))},
        scratch_shapes=[pltpu.SemaphoreType.DMA((len(moves),))],
        compiler_params=kernel_params(),
        cost_estimate=NO_COST,
        name="join",
    )(*sources, *targets)


def gate_kernel(*_):
    pass


def gate(block, *after):
    return pl.pallas_call(
        gate_kernel,
        in_specs=[IN_ANY] * (1 + len(after)),
        out_specs=IN_ANY,
        out_shape=jax.ShapeDtypeStruct(block.shape, block.dtype),
        input_output_aliases={0: 0},
        compiler_params=kernel_params(),
        name="gate",
    )(block, *after)


def staged_groups(along_wa, along_col):
    return (
        (0,),
        *(tuple(range(a * along_col, (a + 1) * along_col)) for a in range(1, along_wa)),
        *((c, *(None,) * (along_wa - 1)) for c in range(1, along_col)),
    )


def stage_along_wa(blocks, along_wa, along_col):
    passed = {a: swap(blocks[a], a * along_col) for a in reversed(range(1, along_wa))}
    return [passed[a] for a in range(1, along_wa)]


def stage_along_col(blocks, first, along_wa, along_col, after):
    second = blocks[along_wa:]
    if first and second:
        moves = tuple(((a - 1, c), (c - 1, a)) for a in range(1, along_wa) for c in range(1, along_col))
        second = join([*first, after], second, moves)
    second = [swap(block, c) for c, block in enumerate(second, 1)]
    where = tuple((along_wa + c - 1, a) if c else (a, 0) for a in range(along_wa) for c in range(along_col))
    return [blocks[0], *first, *second], where


def by_permutes(walkers, intersection_inverse, noise_index, cholesky):
    walker_count = walkers.shape[0]
    tile_rows = cholesky.shape[1]
    planes = lax.axis_size(PLANE)
    along_wa, along_col = lax.axis_size("wa"), lax.axis_size("col")
    half, half_wa = planes // 2, along_wa // 2
    far, near = tuple(range(half, planes)), tuple(range(half))
    early, late = far[:2], far[2:]
    noise = quantile(noise_index)
    direct = tuple((p,) for p in range(planes))
    staged = staged_groups(along_wa, along_col)
    staged_near = staged_groups(half_wa, along_col)

    def make_green(k, groups, after):
        return green_rows(walkers, intersection_inverse, k, tile_rows, groups, True, after)

    def ordered(received):
        places = (*far, *near)
        return [received[p] for p in places], tuple((places.index(p), 0) for p in range(planes))

    split = [(p,) for p in early], [(p,) for p in late]
    one = make_green(0, (*split[0], *staged_near[1:half_wa]), walkers)
    two = make_green(0, (*split[1], staged_near[0], *staged_near[half_wa:]), one[0])
    near_blocks = [two[len(late)], *one[len(early) :], *two[len(late) + 1 :]]
    got_early = [swap(block, p) for p, block in zip(early, one)]
    got_near = stage_along_wa(near_blocks, half_wa, along_col)
    got_late = [swap(block, p) for p, block in zip(late, two)]
    got, where = stage_along_col(near_blocks, got_near, half_wa, along_col, two[0])
    held = load(cholesky, two[0])
    shift = len(far)
    greens = (
        [*got_early, *got_late, *got],
        (*((i + shift, j) for i, j in where), *((i, 0) for i in range(shift))),
        True,
    )
    token = held

    def reduced(sums):
        distance = 1
        while distance < half:
            sums = sums + swap(sums, distance)
            distance *= 2
        sums = [sums]
        for j in range(half_wa):
            pairs = ((0, half_wa + j), (along_wa - 1, half_wa - 1 - j))
            sums.append(lax.ppermute(sums[0], "wa", pairs))
        return sums

    new, log_steps = walkers, []
    waiting = None
    for k in range(walker_count):
        last = k == walker_count - 1
        if not last:
            later = make_green(k + 1, staged, token)
            token = later[0]
            coming = stage_along_wa(later, along_wa, along_col)
        parts = reduced(bias_rows(held, noise[k : k + 1], *greens))
        if waiting is not None:
            first = stage_along_wa(waiting, along_wa, along_col)
        groups = direct if last else staged
        blocks, log_all = potential_rows(parts, held, groups, True, later[0] if last else coming[half_wa - 1])
        log_steps.append(lax.dynamic_index_in_dim(log_all[:, 0], lax.axis_index(PLANE), 0, keepdims=True))
        if waiting is not None:
            new = taylor(
                *stage_along_col(waiting, first, along_wa, along_col, log_all), True, walkers, k - 1, new, walkers
            )
        if last:
            got = {p: swap(block, p) for p, block in enumerate(blocks)}
            new = taylor(*ordered(got), True, walkers, k, new, walkers)
        else:
            waiting = blocks
            greens = (*stage_along_col(later, coming, along_wa, along_col, log_all), True)
    return new, jnp.concatenate(log_steps)


def by_all_to_all(walkers, intersection_inverse, noise_index, cholesky):
    walker_count, orbitals, electrons = walkers.shape
    vectors, tile_rows, _ = cholesky.shape
    planes = lax.axis_size(PLANE)
    green = jnp.einsum(
        "kpe,kef->kpf", walkers, intersection_inverse, preferred_element_type=jnp.float32
    ).astype(jnp.bfloat16)
    green = lax.all_to_all(
        green.reshape(walker_count, planes, tile_rows, electrons), PLANE, split_axis=1, concat_axis=1, tiled=True
    )
    partial_sums = jnp.einsum(
        "kspe,gpe->ksg", green, cholesky[:, :, :electrons], preferred_element_type=jnp.float32
    )
    bias_sum = lax.psum(partial_sums, PLANE)
    noise = lax.all_gather(quantile(noise_index), PLANE, axis=1, tiled=False)
    shifted, log_terms = shifted_field(bias_sum, noise)
    log_weight = lax.dynamic_index_in_dim(jnp.sum(log_terms, axis=-1), lax.axis_index(PLANE), 1, keepdims=False)
    rows = jnp.einsum(
        "ksg,gpq->kspq", shifted.astype(jnp.bfloat16), cholesky, preferred_element_type=jnp.float32
    ).astype(jnp.bfloat16)
    potential = lax.all_to_all(rows, PLANE, split_axis=1, concat_axis=1, tiled=True)
    new = taylor_steps(
        potential.reshape(walker_count, orbitals, orbitals),
        walkers,
        lambda a, b: jnp.einsum("kpq,kqe->kpe", a, b, preferred_element_type=jnp.float32),
    )
    return new, log_weight


def per_device(walkers, intersection_inverse, noise_index, cholesky):
    planes = lax.axis_size(PLANE)
    tile_rows = cholesky.shape[1]
    permutes = 2 <= planes <= MOST_PERMUTES and planes & (planes - 1) == 0 and tile_rows % ROWS == 0
    step = by_permutes if permutes else by_all_to_all
    return step(walkers, intersection_inverse, noise_index, cholesky)


def solution(mesh):
    placed = (
        P(("grp", "wa", "col", "row"), None, None),
        P(("grp", "wa", "col", "row"), None, None),
        P(("grp", "wa", "col", "row"), None),
        P(None, ("wa", "col"), None),
    )
    return jax.shard_map(
        per_device,
        mesh=mesh,
        in_specs=placed,
        out_specs=(P(("grp", "wa", "col", "row"), None, None), P(("grp", "wa", "col", "row"))),
        check_vma=False,
    )
```

```python
import functools
import math

import jax
import jax.numpy as jnp
from jax import lax
from jax.experimental import pallas as pl
from jax.experimental.pallas import tpu as pltpu
from jax.sharding import PartitionSpec as P

NOISE_LEVELS = 65536


STEP_ROOT = 0.1
BIAS_CAP = 1.0
ROOT_TWO = 1.4142135623730951
DEGREES = 4
PLANE = ("wa", "col")
ROWS = 16
MOST_PERMUTES = 8
VMEM = 16 * 1024 * 1024
IN_VMEM = pl.BlockSpec(memory_space=pltpu.VMEM)
IN_SMEM = pl.BlockSpec(memory_space=pltpu.SMEM)
IN_HBM = pl.BlockSpec(memory_space=pltpu.HBM)
IN_ANY = pl.BlockSpec(memory_space=pl.ANY)


NO_COST = pl.CostEstimate(flops=0, bytes_accessed=0, transcendentals=0)


def kernel_params():
    return pltpu.CompilerParams(vmem_limit_bytes=VMEM)


def quantile(codes):
    level = (codes.astype(jnp.float32) + 0.5) / NOISE_LEVELS
    return ROOT_TWO * lax.erf_inv(2.0 * level - 1.0)


def shifted_field(bias_sum, noise):
    force_bias = jnp.clip(STEP_ROOT * bias_sum, -BIAS_CAP, BIAS_CAP)
    shifted = noise - force_bias
    return shifted, shifted * force_bias - 0.5 * force_bias * force_bias


def iota(shape, dimension):
    return lax.broadcasted_iota(jnp.int32, shape, dimension)


def own_place():
    return lax.axis_index("wa") * lax.axis_size("col") + lax.axis_index("col")


def in_vmem(array):
    return pltpu.with_memory_space_constraint(array, pltpu.VMEM)


def in_hbm(array):
    return pltpu.with_memory_space_constraint(array, pltpu.HBM)


def device_at(place, relative):
    return jnp.bitwise_xor(own_place(), place) if relative else place


def green_kernel(k, groups, relative, walker_ref, inverse_ref, _, *refs):
    outs, (rows_in, inverse_in, arrived) = refs[: len(groups)], refs[len(groups) :]
    tile_rows = rows_in.shape[1]
    copies = [pltpu.make_async_copy(inverse_ref.at[k], inverse_in, arrived.at[0])]
    places = [place for place in sum(groups, ()) if place is not None]
    for i, place in enumerate(places):
        start = pl.multiple_of(device_at(place, relative) * tile_rows, tile_rows)
        copies.append(
            pltpu.make_async_copy(
                walker_ref.at[k, pl.ds(start, tile_rows), :], rows_in.at[i], arrived.at[i + 1]
            )
        )
    for copy in copies:
        copy.start()
    for copy in copies:
        copy.wait()
    rows = rows_in[...].reshape(-1, rows_in.shape[2])
    product = jnp.dot(rows, inverse_in[...], preferred_element_type=jnp.float32).astype(jnp.bfloat16)
    i = 0
    for group, out_ref in zip(groups, outs):
        for j, place in enumerate(group):
            if place is not None:
                out_ref[j] = product[i * tile_rows : (i + 1) * tile_rows, :]
                i += 1


def green_rows(walkers, inverses, k, tile_rows, groups, relative, after):
    _, orbitals, electrons = walkers.shape
    count = sum(place is not None for group in groups for place in group)
    return pl.pallas_call(
        functools.partial(green_kernel, k, groups, relative),
        in_specs=[IN_HBM, IN_HBM, IN_ANY],
        out_specs=[IN_VMEM] * len(groups),
        out_shape=[jax.ShapeDtypeStruct((len(group), tile_rows, electrons), jnp.bfloat16) for group in groups],
        scratch_shapes=[
            pltpu.VMEM((count, tile_rows, electrons), jnp.bfloat16),
            pltpu.VMEM((electrons, electrons), jnp.bfloat16),
            pltpu.SemaphoreType.DMA((count + 1,)),
        ],
        compiler_params=kernel_params(),
        cost_estimate=NO_COST,
        name="green_rows",
    )(in_hbm(walkers), in_hbm(inverses), after)


def load_kernel(start, chol_ref, _, held_ref, arrived):
    step = chol_ref.shape[0] // arrived.shape[0]
    columns = pl.ds(start, held_ref.shape[2])
    copies = [
        pltpu.make_async_copy(
            chol_ref.at[pl.ds(i * step, step), :, columns], held_ref.at[pl.ds(i * step, step)], arrived.at[i]
        )
        for i in range(arrived.shape[0])
    ]
    for copy in copies:
        copy.start()
    for copy in copies:
        copy.wait()


def load(cholesky, start, stop, after):
    vectors, tile_rows, _ = cholesky.shape
    return pl.pallas_call(
        functools.partial(load_kernel, start),
        in_specs=[IN_HBM, IN_ANY],
        out_specs=IN_VMEM,
        out_shape=pltpu.VMEM((vectors, tile_rows, stop - start), cholesky.dtype),
        scratch_shapes=[pltpu.SemaphoreType.DMA((math.gcd(vectors, 8),))],
        compiler_params=kernel_params(),
        cost_estimate=NO_COST,
        name="load_cholesky",
    )(in_hbm(cholesky), after)


def bring_kernel(k, walkers_ref, _, held_ref, arrived):
    copy = pltpu.make_async_copy(walkers_ref.at[k], held_ref, arrived)
    copy.start()
    copy.wait()


def bring(walkers, k, after):
    return pl.pallas_call(
        functools.partial(bring_kernel, k),
        in_specs=[IN_HBM, IN_ANY],
        out_specs=IN_VMEM,
        out_shape=pltpu.VMEM(walkers.shape[1:], walkers.dtype),
        scratch_shapes=[pltpu.SemaphoreType.DMA(())],
        compiler_params=kernel_params(),
        cost_estimate=NO_COST,
        name="bring_walker",
    )(in_hbm(walkers), after)


def bias_kernel(where, relative, chol_ref, noise_ref, *refs):
    greens, out_ref = refs[:-1], refs[-1]
    count = len(where)
    vectors, tile_rows, _ = chol_ref.shape
    electrons = greens[0].shape[2]
    me = own_place()
    total = jnp.zeros((vectors * ROWS, count * ROWS), jnp.float32)
    for start in range(0, tile_rows, ROWS):
        green = jnp.concatenate([greens[i][j, start : start + ROWS, :] for i, j in where], axis=0)
        tile = chol_ref[:, start : start + ROWS, :electrons].reshape(vectors * ROWS, electrons)
        total += lax.dot_general(tile, green, (((1,), (1,)), ((), ())), preferred_element_type=jnp.float32)
    total = total.reshape(vectors, ROWS, count * ROWS)
    same = iota(total.shape, 1) == iota(total.shape, 2) % ROWS
    summed = jnp.sum(jnp.where(same, total, 0.0), axis=1)
    shape = (count, count * ROWS)
    source = iota(shape, 1) // ROWS
    fold = (jnp.bitwise_xor(source, me) if relative else source) == iota(shape, 0)
    out_ref[:count, :] = lax.dot_general(
        fold.astype(jnp.float32),
        summed,
        (((1,), (1,)), ((), ())),
        preferred_element_type=jnp.float32,
        precision=lax.Precision.HIGHEST,
    )
    out_ref[count:, :] = jnp.where(iota((count, vectors), 0) == me, noise_ref[...], 0.0)


def bias_rows(cholesky, noise, greens, where, relative):
    vectors, tile_rows, _ = cholesky.shape
    count, electrons = len(where), greens[0].shape[2]
    return pl.pallas_call(
        functools.partial(bias_kernel, where, relative),
        in_specs=[IN_VMEM] * (2 + len(greens)),
        out_specs=IN_VMEM,
        out_shape=jax.ShapeDtypeStruct((2 * count, vectors), jnp.float32),
        compiler_params=kernel_params(),
        cost_estimate=NO_COST,
        name="bias_rows",
    )(cholesky, noise, *greens)


def potential_kernel(groups, relative, parts, pieces, *refs):
    sums, chols, refs = refs[:parts], refs[parts : parts + pieces], refs[parts + pieces :]
    before_ref, outs, log_ref = refs[0], refs[2:-1], refs[-1]
    places = [(place, out_ref, j) for group, out_ref in zip(groups, outs) for j, place in enumerate(group)]
    places = [slot for slot in places if slot[0] is not None]
    count = len(places)
    vectors, tile_rows, _ = chols[0].shape
    totals = [ref[...] for ref in sums]
    total = totals[0] + sum(totals[2:], totals[1])
    shifted, log_terms = shifted_field(total[:count, :], total[count:, :])
    own = iota(log_terms.shape, 0) == own_place()
    known = log_ref.shape[0] - 1
    for i in range(known):
        log_ref[i] = before_ref[i]
    log_ref[known] = jnp.sum(jnp.where(own, log_terms, 0.0))
    field = shifted.astype(jnp.bfloat16)
    if relative:
        order = jnp.bitwise_xor(iota((count, count), 0), own_place()) == iota((count, count), 1)
        field = jnp.dot(order.astype(jnp.bfloat16), field, preferred_element_type=jnp.float32).astype(jnp.bfloat16)
    widen = (iota((vectors, vectors * ROWS), 1) // ROWS == iota((vectors, vectors * ROWS), 0)).astype(jnp.bfloat16)
    wide = jnp.dot(field, widen, preferred_element_type=jnp.float32)
    shape = (count, ROWS, vectors * ROWS)
    spread = jnp.where(iota(shape, 1) == iota(shape, 2) % ROWS, wide[:, None, :], 0.0)
    spread = spread.reshape(count * ROWS, vectors * ROWS).astype(jnp.bfloat16)
    for start in range(0, tile_rows, ROWS):
        column = 0
        for chol_ref in chols:
            width = chol_ref.shape[2]
            tile = chol_ref[:, start : start + ROWS, :].reshape(vectors * ROWS, width)
            rows = jnp.dot(spread, tile, preferred_element_type=jnp.float32).astype(jnp.bfloat16)
            for place, out_ref, j in places:
                out_ref[j, start : start + ROWS, column : column + width] = rows[place * ROWS : (place + 1) * ROWS, :]
            column += width


def potential_rows(sums, cholesky, groups, relative, log_steps, after):
    vectors, tile_rows, _ = cholesky[0].shape
    orbitals = sum(piece.shape[2] for piece in cholesky)
    count = sums[0].shape[0] // 2
    known = 0 if log_steps is None else log_steps.shape[0]
    before = jnp.zeros((1,), jnp.float32) if log_steps is None else log_steps
    *blocks, log_steps = pl.pallas_call(
        functools.partial(potential_kernel, groups, relative, len(sums), len(cholesky)),
        in_specs=[IN_VMEM] * (len(sums) + len(cholesky)) + [IN_SMEM, IN_ANY],
        out_specs=[IN_VMEM] * len(groups) + [IN_SMEM],
        out_shape=[
            *(jax.ShapeDtypeStruct((len(group), tile_rows, orbitals), jnp.bfloat16) for group in groups),
            jax.ShapeDtypeStruct((known + 1,), jnp.float32),
        ],
        compiler_params=kernel_params(),
        cost_estimate=NO_COST,
        name="potential_rows",
    )(*sums, *cholesky, before, after)
    return blocks, log_steps


def taylor_steps(potential, term, product_of):
    running = term.astype(jnp.float32)
    for degree in range(1, DEGREES + 1):
        product = (-STEP_ROOT / degree) * product_of(potential, term)
        running = running + product
        term = product.astype(jnp.bfloat16)
    return running.astype(jnp.bfloat16)


def taylor_kernel(k, where, *refs):
    blocks, (walker_ref, _, _, out_ref, held, terms, running, result, written) = refs[:-9], refs[-9:]
    for place, (i, j) in enumerate(where):
        held[device_at(place, True)] = blocks[i][j]
    count, tile_rows, orbitals = held.shape
    source = walker_ref
    for degree in range(1, DEGREES):
        product = (-STEP_ROOT / degree) * jnp.dot(
            held[...].reshape(orbitals, orbitals), source[...], preferred_element_type=jnp.float32
        )
        source = terms.at[degree % 2]
        source[...] = product.astype(jnp.bfloat16)
        running[...] = product + (walker_ref[...].astype(jnp.float32) if degree == 1 else running[...])
    step = max(count // 4, 1)
    writes = []
    for i in range(count // step):
        rows = pl.ds(i * step * tile_rows, step * tile_rows)
        product = (-STEP_ROOT / DEGREES) * jnp.dot(
            held[i * step : (i + 1) * step].reshape(step * tile_rows, orbitals),
            source[...],
            preferred_element_type=jnp.float32,
        )
        result[rows, :] = (running[rows, :] + product).astype(jnp.bfloat16)
        writes.append(pltpu.make_async_copy(result.at[rows], out_ref.at[k, rows], written.at[i]))
        writes[-1].start()
    for write in writes:
        write.wait()


def taylor(blocks, where, walker, k, new, after):
    orbitals, electrons = walker.shape
    count, tile_rows = len(where), blocks[0].shape[1]
    return pl.pallas_call(
        functools.partial(taylor_kernel, k, where),
        in_specs=[IN_VMEM] * (len(blocks) + 1) + [IN_HBM, IN_ANY],
        out_specs=IN_HBM,
        out_shape=jax.ShapeDtypeStruct(new.shape, jnp.bfloat16),
        scratch_shapes=[
            pltpu.VMEM((count, tile_rows, orbitals), jnp.bfloat16),
            pltpu.VMEM((2, orbitals, electrons), jnp.bfloat16),
            pltpu.VMEM((orbitals, electrons), jnp.float32),
            pltpu.VMEM((orbitals, electrons), jnp.bfloat16),
            pltpu.SemaphoreType.DMA((count,)),
        ],
        input_output_aliases={len(blocks) + 1: 0} if k else {},
        compiler_params=kernel_params(),
        cost_estimate=NO_COST,
        name="taylor",
    )(*(in_vmem(block) for block in blocks), walker, in_hbm(new), after)


def swap(block, place):
    if place == 0:
        return block
    planes = lax.axis_size(PLANE)
    return lax.ppermute(block, PLANE, [(i, i ^ place) for i in range(planes)])


def join_kernel(moves, sources, *refs):
    outs, arrived = refs[-1 - (len(refs) - sources - 1) // 2 : -1], refs[-1]
    copies = [
        pltpu.make_async_copy(refs[i].at[pl.ds(j, 1)], outs[o].at[pl.ds(q, 1)], arrived.at[m])
        for m, ((i, j), (o, q)) in enumerate(moves)
    ]
    for copy in copies:
        copy.start()
    for copy in copies:
        copy.wait()


def join(sources, targets, moves):
    return pl.pallas_call(
        functools.partial(join_kernel, moves, len(sources)),
        in_specs=[IN_ANY] * (len(sources) + len(targets)),
        out_specs=[IN_ANY] * len(targets),
        out_shape=[jax.ShapeDtypeStruct(target.shape, target.dtype) for target in targets],
        input_output_aliases={len(sources) + i: i for i in range(len(targets))},
        scratch_shapes=[pltpu.SemaphoreType.DMA((len(moves),))],
        compiler_params=kernel_params(),
        cost_estimate=NO_COST,
        name="join",
    )(*sources, *targets)


def staged_groups(along_wa, along_col):
    return (
        (0,),
        *(tuple(range(a * along_col, (a + 1) * along_col)) for a in range(1, along_wa)),
        *((c, *(None,) * (along_wa - 1)) for c in range(1, along_col)),
    )


def stage_along_wa(blocks, along_wa, along_col):
    passed = {a: swap(blocks[a], a * along_col) for a in reversed(range(1, along_wa))}
    return [passed[a] for a in range(1, along_wa)]


def stage_along_col(blocks, first, along_wa, along_col, after):
    second = blocks[along_wa:]
    if first and second:
        moves = tuple(((along_wa - 1 - a, c), (c - 1, a)) for a in range(1, along_wa) for c in range(1, along_col))
        second = join([*reversed(first), *after], second, moves)
    second = [swap(block, c) for c, block in enumerate(second, 1)]
    where = tuple((along_wa + c - 1, a) if c else (a, 0) for a in range(along_wa) for c in range(along_col))
    return [blocks[0], *first, *second], where


def by_permutes(walkers, intersection_inverse, noise_index, cholesky):
    walker_count = walkers.shape[0]
    tile_rows = cholesky.shape[1]
    planes = lax.axis_size(PLANE)
    along_wa, along_col = lax.axis_size("wa"), lax.axis_size("col")
    half, half_wa = planes // 2, along_wa // 2
    far, near = tuple(range(half, planes)), tuple(range(half))
    noise = quantile(noise_index)
    direct = tuple((p,) for p in range(planes))
    staged = staged_groups(along_wa, along_col)

    def make_green(k, groups, after):
        return green_rows(walkers, intersection_inverse, k, tile_rows, groups, True, after)

    def ordered(received):
        places = (*near[2:], *far, *near[:2])
        return [received[p] for p in places], tuple((places.index(p), 0) for p in range(planes))

    short = along_wa - 1
    staged_short = staged_groups(short, along_col)
    last_ones = tuple((p,) for p in range(short * along_col, planes))
    one = make_green(0, staged_short[1:short], walkers)
    two = make_green(0, (*last_ones, staged_short[0], *staged_short[short:]), one[0])
    blocks = [two[along_col], *one, *two[along_col + 1 :]]
    orbitals, electrons = walkers.shape[1:]
    cut = orbitals // 2 if orbitals % 256 == 0 and electrons <= orbitals // 2 else orbitals
    held = [load(cholesky, 0, cut, two[0])]
    direct_ones = [swap(block, p) for (p,), block in zip(last_ones, two)]
    passing = stage_along_wa(blocks, short, along_col)
    staged_ones, where = stage_along_col(blocks, passing, short, along_col, held)
    greens = (
        [*direct_ones, *staged_ones],
        (*((i + along_col, j) for i, j in where), *((i, 0) for i in range(along_col))),
        True,
    )
    token = passing[-1]

    def reduced(sums):
        distance = 1
        while distance < half:
            sums = sums + swap(sums, distance)
            distance *= 2
        sums = [sums]
        for j in range(half_wa):
            pairs = ((0, half_wa + j), (along_wa - 1, half_wa - 1 - j))
            sums.append(lax.ppermute(sums[0], "wa", pairs))
        return sums

    new, log_steps = walkers, None
    waiting = None
    for k in range(walker_count):
        last = k == walker_count - 1
        if not last:
            later = make_green(k + 1, staged, token)
            token = later[0]
            coming = stage_along_wa(later, along_wa, along_col)
        sums = bias_rows(held[0], noise[k : k + 1], *greens)
        if k == 0 and cut < orbitals:
            held.append(load(cholesky, cut, orbitals, sums))
        parts = reduced(sums)
        if waiting is not None:
            first = stage_along_wa(waiting, along_wa, along_col)
        groups = direct if last else staged
        after = later[0] if last else coming[half_wa - 1]
        blocks, log_steps = potential_rows(parts, held, groups, True, log_steps, after)
        walker = bring(walkers, k, log_steps)
        got = {p: swap(blocks[p], p) for p in (*near[2:], *far, *near[:2])} if last else {}
        if waiting is not None:
            passed = [walker, before, log_steps]
            new = taylor(*stage_along_col(waiting, first, along_wa, along_col, passed), before, k - 1, new, walkers)
        before = walker
        if last:
            new = taylor(*ordered(got), walker, k, new, walkers)
        else:
            waiting = blocks
            greens = (*stage_along_col(later, coming, along_wa, along_col, [log_steps]), True)
    return new, log_steps


def by_all_to_all(walkers, intersection_inverse, noise_index, cholesky):
    walker_count, orbitals, electrons = walkers.shape
    vectors, tile_rows, _ = cholesky.shape
    planes = lax.axis_size(PLANE)
    green = jnp.einsum(
        "kpe,kef->kpf", walkers, intersection_inverse, preferred_element_type=jnp.float32
    ).astype(jnp.bfloat16)
    green = lax.all_to_all(
        green.reshape(walker_count, planes, tile_rows, electrons), PLANE, split_axis=1, concat_axis=1, tiled=True
    )
    partial_sums = jnp.einsum(
        "kspe,gpe->ksg", green, cholesky[:, :, :electrons], preferred_element_type=jnp.float32
    )
    bias_sum = lax.psum(partial_sums, PLANE)
    noise = lax.all_gather(quantile(noise_index), PLANE, axis=1, tiled=False)
    shifted, log_terms = shifted_field(bias_sum, noise)
    log_weight = lax.dynamic_index_in_dim(jnp.sum(log_terms, axis=-1), lax.axis_index(PLANE), 1, keepdims=False)
    rows = jnp.einsum(
        "ksg,gpq->kspq", shifted.astype(jnp.bfloat16), cholesky, preferred_element_type=jnp.float32
    ).astype(jnp.bfloat16)
    potential = lax.all_to_all(rows, PLANE, split_axis=1, concat_axis=1, tiled=True)
    new = taylor_steps(
        potential.reshape(walker_count, orbitals, orbitals),
        walkers,
        lambda a, b: jnp.einsum("kpq,kqe->kpe", a, b, preferred_element_type=jnp.float32),
    )
    return new, log_weight


def per_device(walkers, intersection_inverse, noise_index, cholesky):
    planes = lax.axis_size(PLANE)
    tile_rows = cholesky.shape[1]
    permutes = 2 <= planes <= MOST_PERMUTES and planes & (planes - 1) == 0 and tile_rows % ROWS == 0
    step = by_permutes if permutes else by_all_to_all
    return step(walkers, intersection_inverse, noise_index, cholesky)


def solution(mesh):
    placed = (
        P(("grp", "wa", "col", "row"), None, None),
        P(("grp", "wa", "col", "row"), None, None),
        P(("grp", "wa", "col", "row"), None),
        P(None, ("wa", "col"), None),
    )
    return jax.shard_map(
        per_device,
        mesh=mesh,
        in_specs=placed,
        out_specs=(P(("grp", "wa", "col", "row"), None, None), P(("grp", "wa", "col", "row"))),
        check_vma=False,
    )
```

```python
import functools
import math

import jax
import jax.numpy as jnp
from jax import lax
from jax.experimental import pallas as pl
from jax.experimental.pallas import tpu as pltpu
from jax.sharding import PartitionSpec as P

NOISE_LEVELS = 65536


STEP_ROOT = 0.1
BIAS_CAP = 1.0
ROOT_TWO = 1.4142135623730951
DEGREES = 4
PLANE = ("wa", "col")
ROWS = 16
MOST_PERMUTES = 8
VMEM = 16 * 1024 * 1024
IN_VMEM = pl.BlockSpec(memory_space=pltpu.VMEM)
IN_SMEM = pl.BlockSpec(memory_space=pltpu.SMEM)
IN_HBM = pl.BlockSpec(memory_space=pltpu.HBM)
IN_ANY = pl.BlockSpec(memory_space=pl.ANY)


NO_COST = pl.CostEstimate(flops=0, bytes_accessed=0, transcendentals=0)


def kernel_params():
    return pltpu.CompilerParams(vmem_limit_bytes=VMEM)


def quantile(codes):
    level = (codes.astype(jnp.float32) + 0.5) / NOISE_LEVELS
    return ROOT_TWO * lax.erf_inv(2.0 * level - 1.0)


def shifted_field(bias_sum, noise):
    force_bias = jnp.clip(STEP_ROOT * bias_sum, -BIAS_CAP, BIAS_CAP)
    shifted = noise - force_bias
    return shifted, shifted * force_bias - 0.5 * force_bias * force_bias


def iota(shape, dimension):
    return lax.broadcasted_iota(jnp.int32, shape, dimension)


def own_place():
    return lax.axis_index("wa") * lax.axis_size("col") + lax.axis_index("col")


def in_vmem(array):
    return pltpu.with_memory_space_constraint(array, pltpu.VMEM)


def in_hbm(array):
    return pltpu.with_memory_space_constraint(array, pltpu.HBM)


def device_at(place, relative):
    return jnp.bitwise_xor(own_place(), place) if relative else place


def green_kernel(k, groups, relative, walker_ref, inverse_ref, _, *refs):
    outs, (rows_in, inverse_in, arrived) = refs[: len(groups)], refs[len(groups) :]
    tile_rows = rows_in.shape[1]
    copies = [pltpu.make_async_copy(inverse_ref.at[k], inverse_in, arrived.at[0])]
    places = [place for place in sum(groups, ()) if place is not None]
    for i, place in enumerate(places):
        start = pl.multiple_of(device_at(place, relative) * tile_rows, tile_rows)
        copies.append(
            pltpu.make_async_copy(
                walker_ref.at[k, pl.ds(start, tile_rows), :], rows_in.at[i], arrived.at[i + 1]
            )
        )
    for copy in copies:
        copy.start()
    for copy in copies:
        copy.wait()
    rows = rows_in[...].reshape(-1, rows_in.shape[2])
    product = jnp.dot(rows, inverse_in[...], preferred_element_type=jnp.float32).astype(jnp.bfloat16)
    i = 0
    for group, out_ref in zip(groups, outs):
        for j, place in enumerate(group):
            if place is not None:
                out_ref[j] = product[i * tile_rows : (i + 1) * tile_rows, :]
                i += 1


def green_rows(walkers, inverses, k, tile_rows, groups, relative, after):
    _, orbitals, electrons = walkers.shape
    count = sum(place is not None for group in groups for place in group)
    return pl.pallas_call(
        functools.partial(green_kernel, k, groups, relative),
        in_specs=[IN_HBM, IN_HBM, IN_ANY],
        out_specs=[IN_VMEM] * len(groups),
        out_shape=[jax.ShapeDtypeStruct((len(group), tile_rows, electrons), jnp.bfloat16) for group in groups],
        scratch_shapes=[
            pltpu.VMEM((count, tile_rows, electrons), jnp.bfloat16),
            pltpu.VMEM((electrons, electrons), jnp.bfloat16),
            pltpu.SemaphoreType.DMA((count + 1,)),
        ],
        compiler_params=kernel_params(),
        cost_estimate=NO_COST,
        name="green_rows",
    )(in_hbm(walkers), in_hbm(inverses), after)


def load_kernel(start, chol_ref, _, held_ref, arrived):
    step = chol_ref.shape[0] // arrived.shape[0]
    columns = pl.ds(start, held_ref.shape[2])
    copies = [
        pltpu.make_async_copy(
            chol_ref.at[pl.ds(i * step, step), :, columns], held_ref.at[pl.ds(i * step, step)], arrived.at[i]
        )
        for i in range(arrived.shape[0])
    ]
    for copy in copies:
        copy.start()
    for copy in copies:
        copy.wait()


def load(cholesky, start, stop, after):
    vectors, tile_rows, _ = cholesky.shape
    return pl.pallas_call(
        functools.partial(load_kernel, start),
        in_specs=[IN_HBM, IN_ANY],
        out_specs=IN_VMEM,
        out_shape=pltpu.VMEM((vectors, tile_rows, stop - start), cholesky.dtype),
        scratch_shapes=[pltpu.SemaphoreType.DMA((math.gcd(vectors, 8),))],
        compiler_params=kernel_params(),
        cost_estimate=NO_COST,
        name="load_cholesky",
    )(in_hbm(cholesky), after)


def bring_kernel(k, walkers_ref, _, held_ref, arrived):
    copy = pltpu.make_async_copy(walkers_ref.at[k], held_ref, arrived)
    copy.start()
    copy.wait()


def bring(walkers, k, after):
    return pl.pallas_call(
        functools.partial(bring_kernel, k),
        in_specs=[IN_HBM, IN_ANY],
        out_specs=IN_VMEM,
        out_shape=pltpu.VMEM(walkers.shape[1:], walkers.dtype),
        scratch_shapes=[pltpu.SemaphoreType.DMA(())],
        compiler_params=kernel_params(),
        cost_estimate=NO_COST,
        name="bring_walker",
    )(in_hbm(walkers), after)


def bias_kernel(where, relative, chol_ref, noise_ref, *refs):
    greens, out_ref = refs[:-1], refs[-1]
    count = len(where)
    vectors, tile_rows, _ = chol_ref.shape
    electrons = greens[0].shape[2]
    me = own_place()
    total = jnp.zeros((vectors * ROWS, count * ROWS), jnp.float32)
    for start in range(0, tile_rows, ROWS):
        green = jnp.concatenate([greens[i][j, start : start + ROWS, :] for i, j in where], axis=0)
        tile = chol_ref[:, start : start + ROWS, :electrons].reshape(vectors * ROWS, electrons)
        total += lax.dot_general(tile, green, (((1,), (1,)), ((), ())), preferred_element_type=jnp.float32)
    total = total.reshape(vectors, ROWS, count * ROWS)
    same = iota(total.shape, 1) == iota(total.shape, 2) % ROWS
    summed = jnp.sum(jnp.where(same, total, 0.0), axis=1)
    shape = (count, count * ROWS)
    source = iota(shape, 1) // ROWS
    fold = (jnp.bitwise_xor(source, me) if relative else source) == iota(shape, 0)
    out_ref[:count, :] = lax.dot_general(
        fold.astype(jnp.float32),
        summed,
        (((1,), (1,)), ((), ())),
        preferred_element_type=jnp.float32,
        precision=lax.Precision.HIGHEST,
    )
    out_ref[count:, :] = jnp.where(iota((count, vectors), 0) == me, noise_ref[...], 0.0)


def bias_rows(cholesky, noise, greens, where, relative):
    vectors, tile_rows, _ = cholesky.shape
    count, electrons = len(where), greens[0].shape[2]
    return pl.pallas_call(
        functools.partial(bias_kernel, where, relative),
        in_specs=[IN_VMEM] * (2 + len(greens)),
        out_specs=IN_VMEM,
        out_shape=jax.ShapeDtypeStruct((2 * count, vectors), jnp.float32),
        compiler_params=kernel_params(),
        cost_estimate=NO_COST,
        name="bias_rows",
    )(cholesky, noise, *greens)


def potential_kernel(groups, relative, parts, pieces, *refs):
    sums, chols, refs = refs[:parts], refs[parts : parts + pieces], refs[parts + pieces :]
    before_ref, outs, log_ref = refs[0], refs[2:-1], refs[-1]
    places = [(place, out_ref, j) for group, out_ref in zip(groups, outs) for j, place in enumerate(group)]
    places = [slot for slot in places if slot[0] is not None]
    count = len(places)
    vectors, tile_rows, _ = chols[0].shape
    totals = [ref[...] for ref in sums]
    total = totals[0] + sum(totals[2:], totals[1])
    shifted, log_terms = shifted_field(total[:count, :], total[count:, :])
    own = iota(log_terms.shape, 0) == own_place()
    known = log_ref.shape[0] - 1
    for i in range(known):
        log_ref[i] = before_ref[i]
    log_ref[known] = jnp.sum(jnp.where(own, log_terms, 0.0))
    field = shifted.astype(jnp.bfloat16)
    if relative:
        order = jnp.bitwise_xor(iota((count, count), 0), own_place()) == iota((count, count), 1)
        field = jnp.dot(order.astype(jnp.bfloat16), field, preferred_element_type=jnp.float32).astype(jnp.bfloat16)
    widen = (iota((vectors, vectors * ROWS), 1) // ROWS == iota((vectors, vectors * ROWS), 0)).astype(jnp.bfloat16)
    wide = jnp.dot(field, widen, preferred_element_type=jnp.float32)
    shape = (count, ROWS, vectors * ROWS)
    spread = jnp.where(iota(shape, 1) == iota(shape, 2) % ROWS, wide[:, None, :], 0.0)
    spread = spread.reshape(count * ROWS, vectors * ROWS).astype(jnp.bfloat16)
    for start in range(0, tile_rows, ROWS):
        column = 0
        for chol_ref in chols:
            width = chol_ref.shape[2]
            tile = chol_ref[:, start : start + ROWS, :].reshape(vectors * ROWS, width)
            rows = jnp.dot(spread, tile, preferred_element_type=jnp.float32).astype(jnp.bfloat16)
            for place, out_ref, j in places:
                out_ref[j, start : start + ROWS, column : column + width] = rows[place * ROWS : (place + 1) * ROWS, :]
            column += width


def potential_rows(sums, cholesky, groups, relative, log_steps, after):
    vectors, tile_rows, _ = cholesky[0].shape
    orbitals = sum(piece.shape[2] for piece in cholesky)
    count = sums[0].shape[0] // 2
    known = 0 if log_steps is None else log_steps.shape[0]
    before = jnp.zeros((1,), jnp.float32) if log_steps is None else log_steps
    *blocks, log_steps = pl.pallas_call(
        functools.partial(potential_kernel, groups, relative, len(sums), len(cholesky)),
        in_specs=[IN_VMEM] * (len(sums) + len(cholesky)) + [IN_SMEM, IN_ANY],
        out_specs=[IN_VMEM] * len(groups) + [IN_SMEM],
        out_shape=[
            *(jax.ShapeDtypeStruct((len(group), tile_rows, orbitals), jnp.bfloat16) for group in groups),
            jax.ShapeDtypeStruct((known + 1,), jnp.float32),
        ],
        compiler_params=kernel_params(),
        cost_estimate=NO_COST,
        name="potential_rows",
    )(*sums, *cholesky, before, after)
    return blocks, log_steps


def taylor_steps(potential, term, product_of):
    running = term.astype(jnp.float32)
    for degree in range(1, DEGREES + 1):
        product = (-STEP_ROOT / degree) * product_of(potential, term)
        running = running + product
        term = product.astype(jnp.bfloat16)
    return running.astype(jnp.bfloat16)


def taylor_kernel(k, where, *refs):
    blocks, (walker_ref, _, _, out_ref, held, terms, running, result, written) = refs[:-9], refs[-9:]
    for place, (i, j) in enumerate(where):
        held[device_at(place, True)] = blocks[i][j]
    count, tile_rows, orbitals = held.shape
    source = walker_ref
    for degree in range(1, DEGREES):
        product = (-STEP_ROOT / degree) * jnp.dot(
            held[...].reshape(orbitals, orbitals), source[...], preferred_element_type=jnp.float32
        )
        source = terms.at[degree % 2]
        source[...] = product.astype(jnp.bfloat16)
        running[...] = product + (walker_ref[...].astype(jnp.float32) if degree == 1 else running[...])
    step = max(count // 4, 1)
    writes = []
    for i in range(count // step):
        rows = pl.ds(i * step * tile_rows, step * tile_rows)
        product = (-STEP_ROOT / DEGREES) * jnp.dot(
            held[i * step : (i + 1) * step].reshape(step * tile_rows, orbitals),
            source[...],
            preferred_element_type=jnp.float32,
        )
        result[rows, :] = (running[rows, :] + product).astype(jnp.bfloat16)
        writes.append(pltpu.make_async_copy(result.at[rows], out_ref.at[k, rows], written.at[i]))
        writes[-1].start()
    for write in writes:
        write.wait()


def taylor(blocks, where, walker, k, new, after):
    orbitals, electrons = walker.shape
    count, tile_rows = len(where), blocks[0].shape[1]
    return pl.pallas_call(
        functools.partial(taylor_kernel, k, where),
        in_specs=[IN_VMEM] * (len(blocks) + 1) + [IN_HBM, IN_ANY],
        out_specs=IN_HBM,
        out_shape=jax.ShapeDtypeStruct(new.shape, jnp.bfloat16),
        scratch_shapes=[
            pltpu.VMEM((count, tile_rows, orbitals), jnp.bfloat16),
            pltpu.VMEM((2, orbitals, electrons), jnp.bfloat16),
            pltpu.VMEM((orbitals, electrons), jnp.float32),
            pltpu.VMEM((orbitals, electrons), jnp.bfloat16),
            pltpu.SemaphoreType.DMA((count,)),
        ],
        input_output_aliases={len(blocks) + 1: 0} if k else {},
        compiler_params=kernel_params(),
        cost_estimate=NO_COST,
        name="taylor",
    )(*(in_vmem(block) for block in blocks), walker, in_hbm(new), after)


def swap(block, place):
    if place == 0:
        return block
    planes = lax.axis_size(PLANE)
    return lax.ppermute(block, PLANE, [(i, i ^ place) for i in range(planes)])


def plus_kernel(a_ref, b_ref, _, out_ref):
    out_ref[...] = a_ref[...] + b_ref[...]


def plus(a, b, after):
    return pl.pallas_call(
        plus_kernel,
        in_specs=[IN_VMEM, IN_VMEM, IN_ANY],
        out_specs=IN_VMEM,
        out_shape=jax.ShapeDtypeStruct(a.shape, a.dtype),
        compiler_params=kernel_params(),
        cost_estimate=NO_COST,
        name="plus",
    )(a, b, after)


def join_kernel(moves, sources, *refs):
    outs, arrived = refs[-1 - (len(refs) - sources - 1) // 2 : -1], refs[-1]
    copies = [
        pltpu.make_async_copy(refs[i].at[pl.ds(j, 1)], outs[o].at[pl.ds(q, 1)], arrived.at[m])
        for m, ((i, j), (o, q)) in enumerate(moves)
    ]
    for copy in copies:
        copy.start()
    for copy in copies:
        copy.wait()


def join(sources, targets, moves):
    return pl.pallas_call(
        functools.partial(join_kernel, moves, len(sources)),
        in_specs=[IN_ANY] * (len(sources) + len(targets)),
        out_specs=[IN_ANY] * len(targets),
        out_shape=[jax.ShapeDtypeStruct(target.shape, target.dtype) for target in targets],
        input_output_aliases={len(sources) + i: i for i in range(len(targets))},
        scratch_shapes=[pltpu.SemaphoreType.DMA((len(moves),))],
        compiler_params=kernel_params(),
        cost_estimate=NO_COST,
        name="join",
    )(*sources, *targets)


def staged_groups(along_wa, along_col):
    return (
        (0,),
        *(tuple(range(a * along_col, (a + 1) * along_col)) for a in range(1, along_wa)),
        *((c, *(None,) * (along_wa - 1)) for c in range(1, along_col)),
    )


def stage_along_wa(blocks, along_wa, along_col):
    passed = {a: swap(blocks[a], a * along_col) for a in reversed(range(1, along_wa))}
    return [passed[a] for a in range(1, along_wa)]


def stage_along_col(blocks, first, along_wa, along_col, after):
    second = blocks[along_wa:]
    if first and second:
        moves = tuple(((along_wa - 1 - a, c), (c - 1, a)) for a in range(1, along_wa) for c in range(1, along_col))
        second = join([*reversed(first), *after], second, moves)
    second = [swap(block, c) for c, block in enumerate(second, 1)]
    where = tuple((along_wa + c - 1, a) if c else (a, 0) for a in range(along_wa) for c in range(along_col))
    return [blocks[0], *first, *second], where


def by_permutes(walkers, intersection_inverse, noise_index, cholesky):
    walker_count = walkers.shape[0]
    tile_rows = cholesky.shape[1]
    planes = lax.axis_size(PLANE)
    along_wa, along_col = lax.axis_size("wa"), lax.axis_size("col")
    half, half_wa = planes // 2, along_wa // 2
    far, near = tuple(range(half, planes)), tuple(range(half))
    noise = quantile(noise_index)
    direct = tuple((p,) for p in range(planes))
    staged = staged_groups(along_wa, along_col)

    def make_green(k, groups, after):
        return green_rows(walkers, intersection_inverse, k, tile_rows, groups, True, after)

    def ordered(received):
        places = (*near[along_col:], *far, *near[:along_col])
        return [received[p] for p in places], tuple((places.index(p), 0) for p in range(planes))

    short = along_wa - 1
    staged_short = staged_groups(short, along_col)
    last_ones = tuple((p,) for p in range(short * along_col, planes))
    one = make_green(0, staged_short[1:short], walkers)
    two = make_green(0, (*last_ones, staged_short[0], *staged_short[short:]), one[0])
    blocks = [two[along_col], *one, *two[along_col + 1 :]]
    orbitals, electrons = walkers.shape[1:]
    cut = orbitals // 2 if orbitals % 512 == 0 and electrons <= orbitals // 2 else orbitals
    held = [load(cholesky, 0, cut, two[0])]
    rest = [(cut, cut + (orbitals - cut) // 2), (cut + (orbitals - cut) // 2, orbitals)] if cut < orbitals else []
    direct_ones = [swap(block, p) for (p,), block in zip(last_ones, two)]
    passing = stage_along_wa(blocks, short, along_col)
    staged_ones, where = stage_along_col(blocks, passing, short, along_col, held)
    greens = (
        [*direct_ones, *staged_ones],
        (*((i + along_col, j) for i, j in where), *((i, 0) for i in range(along_col))),
        True,
    )
    token = passing[-1]

    def reduced(sums):
        distance = 1
        while distance < half:
            if rest:
                held.append(load(cholesky, *rest.pop(0), sums))
            sums = plus(sums, swap(sums, distance), held[-1])
            distance *= 2
        sums = [sums]
        for j in range(half_wa):
            pairs = ((0, half_wa + j), (along_wa - 1, half_wa - 1 - j))
            sums.append(lax.ppermute(sums[0], "wa", pairs))
        return sums

    new, log_steps = walkers, None
    waiting = None
    for k in range(walker_count):
        last = k == walker_count - 1
        if not last:
            later = make_green(k + 1, staged, token)
            token = later[0]
            coming = stage_along_wa(later, along_wa, along_col)
        sums = bias_rows(held[0], noise[k : k + 1], *greens)
        parts = reduced(sums)
        if waiting is not None:
            first = stage_along_wa(waiting, along_wa, along_col)
        groups = direct if last else staged
        after = sums if last else coming[half_wa - 1]
        blocks, log_steps = potential_rows(parts, held, groups, True, log_steps, after)
        walker = bring(walkers, k, log_steps)
        got = {p: swap(blocks[p], p) for p in (*near[along_col:], *far, *near[:along_col])} if last else {}
        if waiting is not None:
            passed = [walker, before, log_steps]
            new = taylor(*stage_along_col(waiting, first, along_wa, along_col, passed), before, k - 1, new, walkers)
        before = walker
        if last:
            new = taylor(*ordered(got), walker, k, new, walkers)
        else:
            waiting = blocks
            greens = (*stage_along_col(later, coming, along_wa, along_col, [log_steps]), True)
    return new, log_steps


def by_all_to_all(walkers, intersection_inverse, noise_index, cholesky):
    walker_count, orbitals, electrons = walkers.shape
    vectors, tile_rows, _ = cholesky.shape
    planes = lax.axis_size(PLANE)
    green = jnp.einsum(
        "kpe,kef->kpf", walkers, intersection_inverse, preferred_element_type=jnp.float32
    ).astype(jnp.bfloat16)
    green = lax.all_to_all(
        green.reshape(walker_count, planes, tile_rows, electrons), PLANE, split_axis=1, concat_axis=1, tiled=True
    )
    partial_sums = jnp.einsum(
        "kspe,gpe->ksg", green, cholesky[:, :, :electrons], preferred_element_type=jnp.float32
    )
    bias_sum = lax.psum(partial_sums, PLANE)
    noise = lax.all_gather(quantile(noise_index), PLANE, axis=1, tiled=False)
    shifted, log_terms = shifted_field(bias_sum, noise)
    log_weight = lax.dynamic_index_in_dim(jnp.sum(log_terms, axis=-1), lax.axis_index(PLANE), 1, keepdims=False)
    rows = jnp.einsum(
        "ksg,gpq->kspq", shifted.astype(jnp.bfloat16), cholesky, preferred_element_type=jnp.float32
    ).astype(jnp.bfloat16)
    potential = lax.all_to_all(rows, PLANE, split_axis=1, concat_axis=1, tiled=True)
    new = taylor_steps(
        potential.reshape(walker_count, orbitals, orbitals),
        walkers,
        lambda a, b: jnp.einsum("kpq,kqe->kpe", a, b, preferred_element_type=jnp.float32),
    )
    return new, log_weight


def per_device(walkers, intersection_inverse, noise_index, cholesky):
    planes = lax.axis_size(PLANE)
    tile_rows = cholesky.shape[1]
    permutes = (
        4 <= lax.axis_size("wa")
        and planes <= MOST_PERMUTES
        and planes & (planes - 1) == 0
        and tile_rows % ROWS == 0
    )
    step = by_permutes if permutes else by_all_to_all
    return step(walkers, intersection_inverse, noise_index, cholesky)


def solution(mesh):
    placed = (
        P(("grp", "wa", "col", "row"), None, None),
        P(("grp", "wa", "col", "row"), None, None),
        P(("grp", "wa", "col", "row"), None),
        P(None, ("wa", "col"), None),
    )
    return jax.shard_map(
        per_device,
        mesh=mesh,
        in_specs=placed,
        out_specs=(P(("grp", "wa", "col", "row"), None, None), P(("grp", "wa", "col", "row"))),
        check_vma=False,
    )
```

```python
import functools
import math

import jax
import jax.numpy as jnp
from jax import lax
from jax.experimental import pallas as pl
from jax.experimental.pallas import tpu as pltpu
from jax.sharding import PartitionSpec as P

NOISE_LEVELS = 65536


STEP_ROOT = 0.1
BIAS_CAP = 1.0
ROOT_TWO = 1.4142135623730951
DEGREES = 4
PLANE = ("wa", "col")
ROWS = 16
MOST_PERMUTES = 8
VMEM = 16 * 1024 * 1024
IN_VMEM = pl.BlockSpec(memory_space=pltpu.VMEM)
IN_SMEM = pl.BlockSpec(memory_space=pltpu.SMEM)
IN_HBM = pl.BlockSpec(memory_space=pltpu.HBM)
IN_ANY = pl.BlockSpec(memory_space=pl.ANY)


NO_COST = pl.CostEstimate(flops=0, bytes_accessed=0, transcendentals=0)


def kernel_params():
    return pltpu.CompilerParams(vmem_limit_bytes=VMEM)


def quantile(codes):
    level = (codes.astype(jnp.float32) + 0.5) / NOISE_LEVELS
    return ROOT_TWO * lax.erf_inv(2.0 * level - 1.0)


def shifted_field(bias_sum, noise):
    force_bias = jnp.clip(STEP_ROOT * bias_sum, -BIAS_CAP, BIAS_CAP)
    shifted = noise - force_bias
    return shifted, shifted * force_bias - 0.5 * force_bias * force_bias


def iota(shape, dimension):
    return lax.broadcasted_iota(jnp.int32, shape, dimension)


def own_place():
    return lax.axis_index("wa") * lax.axis_size("col") + lax.axis_index("col")


def in_vmem(array):
    return pltpu.with_memory_space_constraint(array, pltpu.VMEM)


def in_hbm(array):
    return pltpu.with_memory_space_constraint(array, pltpu.HBM)


def device_at(place, relative):
    return jnp.bitwise_xor(own_place(), place) if relative else place


def green_kernel(k, groups, relative, walker_ref, inverse_ref, _, *refs):
    outs, (rows_in, inverse_in, arrived) = refs[: len(groups)], refs[len(groups) :]
    tile_rows = rows_in.shape[1]
    copies = [pltpu.make_async_copy(inverse_ref.at[k], inverse_in, arrived.at[0])]
    places = [place for place in sum(groups, ()) if place is not None]
    for i, place in enumerate(places):
        start = pl.multiple_of(device_at(place, relative) * tile_rows, tile_rows)
        copies.append(
            pltpu.make_async_copy(
                walker_ref.at[k, pl.ds(start, tile_rows), :], rows_in.at[i], arrived.at[i + 1]
            )
        )
    for copy in copies:
        copy.start()
    for copy in copies:
        copy.wait()
    rows = rows_in[...].reshape(-1, rows_in.shape[2])
    product = jnp.dot(rows, inverse_in[...], preferred_element_type=jnp.float32).astype(jnp.bfloat16)
    i = 0
    for group, out_ref in zip(groups, outs):
        for j, place in enumerate(group):
            if place is not None:
                out_ref[j] = product[i * tile_rows : (i + 1) * tile_rows, :]
                i += 1


def green_rows(walkers, inverses, k, tile_rows, groups, relative, after):
    _, orbitals, electrons = walkers.shape
    count = sum(place is not None for group in groups for place in group)
    return pl.pallas_call(
        functools.partial(green_kernel, k, groups, relative),
        in_specs=[IN_HBM, IN_HBM, IN_ANY],
        out_specs=[IN_VMEM] * len(groups),
        out_shape=[jax.ShapeDtypeStruct((len(group), tile_rows, electrons), jnp.bfloat16) for group in groups],
        scratch_shapes=[
            pltpu.VMEM((count, tile_rows, electrons), jnp.bfloat16),
            pltpu.VMEM((electrons, electrons), jnp.bfloat16),
            pltpu.SemaphoreType.DMA((count + 1,)),
        ],
        compiler_params=kernel_params(),
        cost_estimate=NO_COST,
        name="green_rows",
    )(in_hbm(walkers), in_hbm(inverses), after)


def load_kernel(start, chol_ref, _, held_ref, arrived):
    step = chol_ref.shape[0] // arrived.shape[0]
    columns = pl.ds(start, held_ref.shape[2])
    copies = [
        pltpu.make_async_copy(
            chol_ref.at[pl.ds(i * step, step), :, columns], held_ref.at[pl.ds(i * step, step)], arrived.at[i]
        )
        for i in range(arrived.shape[0])
    ]
    for copy in copies:
        copy.start()
    for copy in copies:
        copy.wait()


def load(cholesky, start, stop, after):
    vectors, tile_rows, _ = cholesky.shape
    return pl.pallas_call(
        functools.partial(load_kernel, start),
        in_specs=[IN_HBM, IN_ANY],
        out_specs=IN_VMEM,
        out_shape=pltpu.VMEM((vectors, tile_rows, stop - start), cholesky.dtype),
        scratch_shapes=[pltpu.SemaphoreType.DMA((math.gcd(vectors, 8),))],
        compiler_params=kernel_params(),
        cost_estimate=NO_COST,
        name="load_cholesky",
    )(in_hbm(cholesky), after)


def bring_kernel(k, walkers_ref, _, held_ref, read, arrived):
    copy = pltpu.make_async_copy(walkers_ref.at[k], read, arrived)
    copy.start()
    copy.wait()
    held_ref[...] = read[...].T


def bring(walkers, k, after):
    _, orbitals, electrons = walkers.shape
    return pl.pallas_call(
        functools.partial(bring_kernel, k),
        in_specs=[IN_HBM, IN_ANY],
        out_specs=IN_VMEM,
        out_shape=pltpu.VMEM((electrons, orbitals), walkers.dtype),
        scratch_shapes=[pltpu.VMEM((orbitals, electrons), walkers.dtype), pltpu.SemaphoreType.DMA(())],
        compiler_params=kernel_params(),
        cost_estimate=NO_COST,
        name="bring_walker",
    )(in_hbm(walkers), after)


def bias_kernel(where, relative, chol_ref, noise_ref, *refs):
    greens, out_ref = refs[:-1], refs[-1]
    count = len(where)
    vectors, tile_rows, _ = chol_ref.shape
    electrons = greens[0].shape[2]
    me = own_place()
    total = jnp.zeros((vectors * ROWS, count * ROWS), jnp.float32)
    for start in range(0, tile_rows, ROWS):
        green = jnp.concatenate([greens[i][j, start : start + ROWS, :] for i, j in where], axis=0)
        tile = chol_ref[:, start : start + ROWS, :electrons].reshape(vectors * ROWS, electrons)
        total += lax.dot_general(tile, green, (((1,), (1,)), ((), ())), preferred_element_type=jnp.float32)
    total = total.reshape(vectors, ROWS, count * ROWS)
    same = iota(total.shape, 1) == iota(total.shape, 2) % ROWS
    summed = jnp.sum(jnp.where(same, total, 0.0), axis=1)
    shape = (count, count * ROWS)
    source = iota(shape, 1) // ROWS
    fold = (jnp.bitwise_xor(source, me) if relative else source) == iota(shape, 0)
    out_ref[:count, :] = lax.dot_general(
        fold.astype(jnp.float32),
        summed,
        (((1,), (1,)), ((), ())),
        preferred_element_type=jnp.float32,
        precision=lax.Precision.HIGHEST,
    )
    out_ref[count:, :] = jnp.where(iota((count, vectors), 0) == me, noise_ref[...], 0.0)


def bias_rows(cholesky, noise, greens, where, relative):
    vectors, tile_rows, _ = cholesky.shape
    count, electrons = len(where), greens[0].shape[2]
    return pl.pallas_call(
        functools.partial(bias_kernel, where, relative),
        in_specs=[IN_VMEM] * (2 + len(greens)),
        out_specs=IN_VMEM,
        out_shape=jax.ShapeDtypeStruct((2 * count, vectors), jnp.float32),
        compiler_params=kernel_params(),
        cost_estimate=NO_COST,
        name="bias_rows",
    )(cholesky, noise, *greens)


def potential_kernel(groups, relative, parts, pieces, *refs):
    sums, chols, refs = refs[:parts], refs[parts : parts + pieces], refs[parts + pieces :]
    before_ref, outs, log_ref = refs[0], refs[2:-1], refs[-1]
    places = [(place, out_ref, j) for group, out_ref in zip(groups, outs) for j, place in enumerate(group)]
    places = [slot for slot in places if slot[0] is not None]
    count = len(places)
    vectors, tile_rows, _ = chols[0].shape
    totals = [ref[...] for ref in sums]
    total = totals[0] + sum(totals[2:], totals[1])
    shifted, log_terms = shifted_field(total[:count, :], total[count:, :])
    own = iota(log_terms.shape, 0) == own_place()
    known = log_ref.shape[0] - 1
    for i in range(known):
        log_ref[i] = before_ref[i]
    log_ref[known] = jnp.sum(jnp.where(own, log_terms, 0.0))
    field = shifted.astype(jnp.bfloat16)
    if relative:
        order = jnp.bitwise_xor(iota((count, count), 0), own_place()) == iota((count, count), 1)
        field = jnp.dot(order.astype(jnp.bfloat16), field, preferred_element_type=jnp.float32).astype(jnp.bfloat16)
    widen = (iota((vectors, vectors * ROWS), 1) // ROWS == iota((vectors, vectors * ROWS), 0)).astype(jnp.bfloat16)
    wide = jnp.dot(field, widen, preferred_element_type=jnp.float32)
    shape = (count, ROWS, vectors * ROWS)
    spread = jnp.where(iota(shape, 1) == iota(shape, 2) % ROWS, wide[:, None, :], 0.0)
    spread = spread.reshape(count * ROWS, vectors * ROWS).astype(jnp.bfloat16)
    for start in range(0, tile_rows, ROWS):
        column = 0
        for chol_ref in chols:
            width = chol_ref.shape[2]
            tile = chol_ref[:, start : start + ROWS, :].reshape(vectors * ROWS, width)
            rows = jnp.dot(spread, tile, preferred_element_type=jnp.float32).astype(jnp.bfloat16)
            for place, out_ref, j in places:
                out_ref[j, start : start + ROWS, column : column + width] = rows[place * ROWS : (place + 1) * ROWS, :]
            column += width


def potential_rows(sums, cholesky, groups, relative, log_steps, after):
    vectors, tile_rows, _ = cholesky[0].shape
    orbitals = sum(piece.shape[2] for piece in cholesky)
    count = sums[0].shape[0] // 2
    known = 0 if log_steps is None else log_steps.shape[0]
    before = jnp.zeros((1,), jnp.float32) if log_steps is None else log_steps
    *blocks, log_steps = pl.pallas_call(
        functools.partial(potential_kernel, groups, relative, len(sums), len(cholesky)),
        in_specs=[IN_VMEM] * (len(sums) + len(cholesky)) + [IN_SMEM, IN_ANY],
        out_specs=[IN_VMEM] * len(groups) + [IN_SMEM],
        out_shape=[
            *(jax.ShapeDtypeStruct((len(group), tile_rows, orbitals), jnp.bfloat16) for group in groups),
            jax.ShapeDtypeStruct((known + 1,), jnp.float32),
        ],
        compiler_params=kernel_params(),
        cost_estimate=NO_COST,
        name="potential_rows",
    )(*sums, *cholesky, before, after)
    return blocks, log_steps


def taylor_steps(potential, term, product_of):
    running = term.astype(jnp.float32)
    for degree in range(1, DEGREES + 1):
        product = (-STEP_ROOT / degree) * product_of(potential, term)
        running = running + product
        term = product.astype(jnp.bfloat16)
    return running.astype(jnp.bfloat16)


def taylor_kernel(k, where, *refs):
    blocks, (walker_ref, _, _, out_ref, held, terms, running, result, written) = refs[:-9], refs[-9:]
    for place, (i, j) in enumerate(where):
        held[device_at(place, True)] = blocks[i][j]
    count, tile_rows, orbitals = held.shape

    def product(degree, term, tiles):
        rows = held[tiles].reshape(-1, orbitals)
        return (-STEP_ROOT / degree) * lax.dot_general(
            term, rows, (((1,), (1,)), ((), ())), preferred_element_type=jnp.float32
        )

    source = walker_ref
    for degree in range(1, DEGREES):
        grown = product(degree, source[...], slice(None))
        source = terms.at[degree % 2]
        source[...] = grown.astype(jnp.bfloat16)
        running[...] = grown + (walker_ref[...].astype(jnp.float32) if degree == 1 else running[...])
    step = max(count // 4, 1)
    writes = []
    for i in range(count // step):
        rows = pl.ds(i * step * tile_rows, step * tile_rows)
        grown = running[:, rows] + product(DEGREES, source[...], slice(i * step, (i + 1) * step))
        result[rows, :] = grown.T.astype(jnp.bfloat16)
        writes.append(pltpu.make_async_copy(result.at[rows], out_ref.at[k, rows], written.at[i]))
        writes[-1].start()
    for write in writes:
        write.wait()


def taylor(blocks, where, walker, k, new, after):
    electrons, orbitals = walker.shape
    count, tile_rows = len(where), blocks[0].shape[1]
    return pl.pallas_call(
        functools.partial(taylor_kernel, k, where),
        in_specs=[IN_VMEM] * (len(blocks) + 1) + [IN_HBM, IN_ANY],
        out_specs=IN_HBM,
        out_shape=jax.ShapeDtypeStruct(new.shape, jnp.bfloat16),
        scratch_shapes=[
            pltpu.VMEM((count, tile_rows, orbitals), jnp.bfloat16),
            pltpu.VMEM((2, electrons, orbitals), jnp.bfloat16),
            pltpu.VMEM((electrons, orbitals), jnp.float32),
            pltpu.VMEM((orbitals, electrons), jnp.bfloat16),
            pltpu.SemaphoreType.DMA((count,)),
        ],
        input_output_aliases={len(blocks) + 1: 0} if k else {},
        compiler_params=kernel_params(),
        cost_estimate=NO_COST,
        name="taylor",
    )(*(in_vmem(block) for block in blocks), walker, in_hbm(new), after)


def swap(block, place):
    if place == 0:
        return block
    planes = lax.axis_size(PLANE)
    return lax.ppermute(block, PLANE, [(i, i ^ place) for i in range(planes)])


def plus_kernel(a_ref, b_ref, *refs):
    refs[-1][...] = a_ref[...] + b_ref[...]


def plus(a, b, after):
    return pl.pallas_call(
        plus_kernel,
        in_specs=[IN_VMEM, IN_VMEM] + [IN_ANY] * len(after),
        out_specs=IN_VMEM,
        out_shape=jax.ShapeDtypeStruct(a.shape, a.dtype),
        compiler_params=kernel_params(),
        cost_estimate=NO_COST,
        name="plus",
    )(a, b, *after)


def join_kernel(moves, sources, *refs):
    outs, arrived = refs[-1 - (len(refs) - sources - 1) // 2 : -1], refs[-1]
    copies = [
        pltpu.make_async_copy(refs[i].at[pl.ds(j, 1)], outs[o].at[pl.ds(q, 1)], arrived.at[m])
        for m, ((i, j), (o, q)) in enumerate(moves)
    ]
    for copy in copies:
        copy.start()
    for copy in copies:
        copy.wait()


def join(sources, targets, moves):
    return pl.pallas_call(
        functools.partial(join_kernel, moves, len(sources)),
        in_specs=[IN_ANY] * (len(sources) + len(targets)),
        out_specs=[IN_ANY] * len(targets),
        out_shape=[jax.ShapeDtypeStruct(target.shape, target.dtype) for target in targets],
        input_output_aliases={len(sources) + i: i for i in range(len(targets))},
        scratch_shapes=[pltpu.SemaphoreType.DMA((len(moves),))],
        compiler_params=kernel_params(),
        cost_estimate=NO_COST,
        name="join",
    )(*sources, *targets)


def staged_groups(along_wa, along_col):
    return (
        (0,),
        *(tuple(range(a * along_col, (a + 1) * along_col)) for a in range(1, along_wa)),
        *((c, *(None,) * (along_wa - 1)) for c in range(1, along_col)),
    )


def stage_along_wa(blocks, along_wa, along_col):
    passed = {a: swap(blocks[a], a * along_col) for a in reversed(range(1, along_wa))}
    return [passed[a] for a in range(1, along_wa)]


def stage_along_col(blocks, first, along_wa, along_col, after):
    second = blocks[along_wa:]
    if first and second:
        moves = tuple(((along_wa - 1 - a, c), (c - 1, a)) for a in range(1, along_wa) for c in range(1, along_col))
        second = join([*reversed(first), *after], second, moves)
    second = [swap(block, c) for c, block in enumerate(second, 1)]
    where = tuple((along_wa + c - 1, a) if c else (a, 0) for a in range(along_wa) for c in range(along_col))
    return [blocks[0], *first, *second], where


def by_permutes(walkers, intersection_inverse, noise_index, cholesky):
    walker_count = walkers.shape[0]
    tile_rows = cholesky.shape[1]
    planes = lax.axis_size(PLANE)
    along_wa, along_col = lax.axis_size("wa"), lax.axis_size("col")
    half, half_wa = planes // 2, along_wa // 2
    far, near = tuple(range(half, planes)), tuple(range(half))
    noise = quantile(noise_index)
    direct = tuple((p,) for p in range(planes))
    staged = staged_groups(along_wa, along_col)

    def make_green(k, groups, after):
        return green_rows(walkers, intersection_inverse, k, tile_rows, groups, True, after)

    def ordered(received):
        places = (*near[along_col:], *far, *near[:along_col])
        return [received[p] for p in places], tuple((places.index(p), 0) for p in range(planes))

    short = along_wa - 1
    staged_short = staged_groups(short, along_col)
    last_ones = tuple((p,) for p in range(short * along_col, planes))
    one = make_green(0, staged_short[1:short], walkers)
    two = make_green(0, (*last_ones, staged_short[0], *staged_short[short:]), one[0])
    blocks = [two[along_col], *one, *two[along_col + 1 :]]
    orbitals, electrons = walkers.shape[1:]
    cut = orbitals // 2 if orbitals % 512 == 0 and electrons <= orbitals // 2 else orbitals
    held = [load(cholesky, 0, cut, two[0])]
    rest = [(cut, cut + (orbitals - cut) // 2), (cut + (orbitals - cut) // 2, orbitals)] if cut < orbitals else []
    direct_ones = [swap(block, p) for (p,), block in zip(last_ones, two)]
    passing = stage_along_wa(blocks, short, along_col)
    staged_ones, where = stage_along_col(blocks, passing, short, along_col, held)
    greens = (
        [*direct_ones, *staged_ones],
        (*((i + along_col, j) for i, j in where), *((i, 0) for i in range(along_col))),
        True,
    )
    token = passing[-1]

    def reduced(sums, wanted):
        distance = 1
        while distance < half:
            if rest:
                held.append(load(cholesky, *rest.pop(0), sums))
            if 2 * distance == half:
                brought.update({i: bring(walkers, i, sums) for i in wanted})
            sums = plus(sums, swap(sums, distance), [held[-1], *brought.values()])
            distance *= 2
        sums = [sums]
        for j in range(half_wa):
            pairs = ((0, half_wa + j), (along_wa - 1, half_wa - 1 - j))
            sums.append(lax.ppermute(sums[0], "wa", pairs))
        return sums

    new, log_steps, brought = walkers, None, {}
    waiting = None
    for k in range(walker_count):
        last = k == walker_count - 1
        if not last:
            later = make_green(k + 1, staged, token)
            token = later[0]
            coming = stage_along_wa(later, along_wa, along_col)
        sums = bias_rows(held[0], noise[k : k + 1], *greens)
        wanted = [i for i in (k - 1, k) if 0 <= i and (i < k or last)]
        parts = reduced(sums, wanted)
        if waiting is not None:
            first = stage_along_wa(waiting, along_wa, along_col)
        groups = direct if last else staged
        after = sums if last else coming[half_wa - 1]
        blocks, log_steps = potential_rows(parts, held, groups, True, log_steps, after)
        got = {p: swap(blocks[p], p) for p in (*near[along_col:], *far, *near[:along_col])} if last else {}
        if waiting is not None:
            passed = [log_steps]
            new = taylor(*stage_along_col(waiting, first, along_wa, along_col, passed), brought.pop(k - 1), k - 1, new, walkers)
        if last:
            new = taylor(*ordered(got), brought[k], k, new, walkers)
        else:
            waiting = blocks
            greens = (*stage_along_col(later, coming, along_wa, along_col, [log_steps]), True)
    return new, log_steps


def by_all_to_all(walkers, intersection_inverse, noise_index, cholesky):
    walker_count, orbitals, electrons = walkers.shape
    vectors, tile_rows, _ = cholesky.shape
    planes = lax.axis_size(PLANE)
    green = jnp.einsum(
        "kpe,kef->kpf", walkers, intersection_inverse, preferred_element_type=jnp.float32
    ).astype(jnp.bfloat16)
    green = lax.all_to_all(
        green.reshape(walker_count, planes, tile_rows, electrons), PLANE, split_axis=1, concat_axis=1, tiled=True
    )
    partial_sums = jnp.einsum(
        "kspe,gpe->ksg", green, cholesky[:, :, :electrons], preferred_element_type=jnp.float32
    )
    bias_sum = lax.psum(partial_sums, PLANE)
    noise = lax.all_gather(quantile(noise_index), PLANE, axis=1, tiled=False)
    shifted, log_terms = shifted_field(bias_sum, noise)
    log_weight = lax.dynamic_index_in_dim(jnp.sum(log_terms, axis=-1), lax.axis_index(PLANE), 1, keepdims=False)
    rows = jnp.einsum(
        "ksg,gpq->kspq", shifted.astype(jnp.bfloat16), cholesky, preferred_element_type=jnp.float32
    ).astype(jnp.bfloat16)
    potential = lax.all_to_all(rows, PLANE, split_axis=1, concat_axis=1, tiled=True)
    new = taylor_steps(
        potential.reshape(walker_count, orbitals, orbitals),
        walkers,
        lambda a, b: jnp.einsum("kpq,kqe->kpe", a, b, preferred_element_type=jnp.float32),
    )
    return new, log_weight


def per_device(walkers, intersection_inverse, noise_index, cholesky):
    planes = lax.axis_size(PLANE)
    tile_rows = cholesky.shape[1]
    permutes = (
        4 <= lax.axis_size("wa")
        and planes <= MOST_PERMUTES
        and planes & (planes - 1) == 0
        and tile_rows % ROWS == 0
    )
    step = by_permutes if permutes else by_all_to_all
    return step(walkers, intersection_inverse, noise_index, cholesky)


def solution(mesh):
    placed = (
        P(("grp", "wa", "col", "row"), None, None),
        P(("grp", "wa", "col", "row"), None, None),
        P(("grp", "wa", "col", "row"), None),
        P(None, ("wa", "col"), None),
    )
    return jax.shard_map(
        per_device,
        mesh=mesh,
        in_specs=placed,
        out_specs=(P(("grp", "wa", "col", "row"), None, None), P(("grp", "wa", "col", "row"))),
        check_vma=False,
    )
```

```python
import functools
import math

import jax
import jax.numpy as jnp
from jax import lax
from jax.experimental import pallas as pl
from jax.experimental.pallas import tpu as pltpu
from jax.sharding import PartitionSpec as P

NOISE_LEVELS = 65536


STEP_ROOT = 0.1
BIAS_CAP = 1.0
ROOT_TWO = 1.4142135623730951
DEGREES = 4
PLANE = ("wa", "col")
ROWS = 16
MOST_PERMUTES = 8
VMEM = 16 * 1024 * 1024
IN_VMEM = pl.BlockSpec(memory_space=pltpu.VMEM)
IN_SMEM = pl.BlockSpec(memory_space=pltpu.SMEM)
IN_HBM = pl.BlockSpec(memory_space=pltpu.HBM)
IN_ANY = pl.BlockSpec(memory_space=pl.ANY)


NO_COST = pl.CostEstimate(flops=0, bytes_accessed=0, transcendentals=0)


def kernel_params():
    return pltpu.CompilerParams(vmem_limit_bytes=VMEM)


def quantile(codes):
    level = (codes.astype(jnp.float32) + 0.5) / NOISE_LEVELS
    return ROOT_TWO * lax.erf_inv(2.0 * level - 1.0)


def shifted_field(bias_sum, noise):
    force_bias = jnp.clip(STEP_ROOT * bias_sum, -BIAS_CAP, BIAS_CAP)
    shifted = noise - force_bias
    return shifted, shifted * force_bias - 0.5 * force_bias * force_bias


def iota(shape, dimension):
    return lax.broadcasted_iota(jnp.int32, shape, dimension)


def own_place():
    return lax.axis_index("wa") * lax.axis_size("col") + lax.axis_index("col")


def in_vmem(array):
    return pltpu.with_memory_space_constraint(array, pltpu.VMEM)


def in_hbm(array):
    return pltpu.with_memory_space_constraint(array, pltpu.HBM)


def device_at(place, relative):
    return jnp.bitwise_xor(own_place(), place) if relative else place


def green_kernel(k, groups, relative, walker_ref, inverse_ref, _, *refs):
    outs, (rows_in, inverse_in, arrived) = refs[: len(groups)], refs[len(groups) :]
    tile_rows = rows_in.shape[1]
    copies = [pltpu.make_async_copy(inverse_ref.at[k], inverse_in, arrived.at[0])]
    places = [place for place in sum(groups, ()) if place is not None]
    for i, place in enumerate(places):
        start = pl.multiple_of(device_at(place, relative) * tile_rows, tile_rows)
        copies.append(
            pltpu.make_async_copy(
                walker_ref.at[k, pl.ds(start, tile_rows), :], rows_in.at[i], arrived.at[i + 1]
            )
        )
    for copy in copies:
        copy.start()
    for copy in copies:
        copy.wait()
    rows = rows_in[...].reshape(-1, rows_in.shape[2])
    product = jnp.dot(rows, inverse_in[...], preferred_element_type=jnp.float32).astype(jnp.bfloat16)
    i = 0
    for group, out_ref in zip(groups, outs):
        for j, place in enumerate(group):
            if place is not None:
                out_ref[j] = product[i * tile_rows : (i + 1) * tile_rows, :]
                i += 1


def green_rows(walkers, inverses, k, tile_rows, groups, relative, after):
    _, orbitals, electrons = walkers.shape
    count = sum(place is not None for group in groups for place in group)
    return pl.pallas_call(
        functools.partial(green_kernel, k, groups, relative),
        in_specs=[IN_HBM, IN_HBM, IN_ANY],
        out_specs=[IN_VMEM] * len(groups),
        out_shape=[jax.ShapeDtypeStruct((len(group), tile_rows, electrons), jnp.bfloat16) for group in groups],
        scratch_shapes=[
            pltpu.VMEM((count, tile_rows, electrons), jnp.bfloat16),
            pltpu.VMEM((electrons, electrons), jnp.bfloat16),
            pltpu.SemaphoreType.DMA((count + 1,)),
        ],
        compiler_params=kernel_params(),
        cost_estimate=NO_COST,
        name="green_rows",
    )(in_hbm(walkers), in_hbm(inverses), after)


def load_kernel(start, chol_ref, _, held_ref, arrived):
    step = chol_ref.shape[0] // arrived.shape[0]
    columns = pl.ds(start, held_ref.shape[2])
    copies = [
        pltpu.make_async_copy(
            chol_ref.at[pl.ds(i * step, step), :, columns], held_ref.at[pl.ds(i * step, step)], arrived.at[i]
        )
        for i in range(arrived.shape[0])
    ]
    for copy in copies:
        copy.start()
    for copy in copies:
        copy.wait()


def load(cholesky, start, stop, after):
    vectors, tile_rows, _ = cholesky.shape
    return pl.pallas_call(
        functools.partial(load_kernel, start),
        in_specs=[IN_HBM, IN_ANY],
        out_specs=IN_VMEM,
        out_shape=pltpu.VMEM((vectors, tile_rows, stop - start), cholesky.dtype),
        scratch_shapes=[pltpu.SemaphoreType.DMA((math.gcd(vectors, 8),))],
        compiler_params=kernel_params(),
        cost_estimate=NO_COST,
        name="load_cholesky",
    )(in_hbm(cholesky), after)


def bring_kernel(k, walkers_ref, _, held_ref, read, arrived):
    copy = pltpu.make_async_copy(walkers_ref.at[k], read, arrived)
    copy.start()
    copy.wait()
    held_ref[...] = read[...].T


def bring(walkers, k, after):
    _, orbitals, electrons = walkers.shape
    return pl.pallas_call(
        functools.partial(bring_kernel, k),
        in_specs=[IN_HBM, IN_ANY],
        out_specs=IN_VMEM,
        out_shape=pltpu.VMEM((electrons, orbitals), walkers.dtype),
        scratch_shapes=[pltpu.VMEM((orbitals, electrons), walkers.dtype), pltpu.SemaphoreType.DMA(())],
        compiler_params=kernel_params(),
        cost_estimate=NO_COST,
        name="bring_walker",
    )(in_hbm(walkers), after)


def bias_kernel(where, relative, chol_ref, noise_ref, *refs):
    greens, out_ref = refs[:-1], refs[-1]
    count = len(where)
    vectors, tile_rows, _ = chol_ref.shape
    electrons = greens[0].shape[2]
    me = own_place()
    total = jnp.zeros((vectors * ROWS, count * ROWS), jnp.float32)
    for start in range(0, tile_rows, ROWS):
        green = jnp.concatenate([greens[i][j, start : start + ROWS, :] for i, j in where], axis=0)
        tile = chol_ref[:, start : start + ROWS, :electrons].reshape(vectors * ROWS, electrons)
        total += lax.dot_general(tile, green, (((1,), (1,)), ((), ())), preferred_element_type=jnp.float32)
    total = total.reshape(vectors, ROWS, count * ROWS)
    same = iota(total.shape, 1) == iota(total.shape, 2) % ROWS
    summed = jnp.sum(jnp.where(same, total, 0.0), axis=1)
    shape = (count, count * ROWS)
    source = iota(shape, 1) // ROWS
    fold = (jnp.bitwise_xor(source, me) if relative else source) == iota(shape, 0)
    out_ref[:count, :] = lax.dot_general(
        fold.astype(jnp.float32),
        summed,
        (((1,), (1,)), ((), ())),
        preferred_element_type=jnp.float32,
        precision=lax.Precision.HIGHEST,
    )
    out_ref[count:, :] = jnp.where(iota((count, vectors), 0) == me, noise_ref[...], 0.0)


def bias_rows(cholesky, noise, greens, where, relative):
    vectors, tile_rows, _ = cholesky.shape
    count, electrons = len(where), greens[0].shape[2]
    return pl.pallas_call(
        functools.partial(bias_kernel, where, relative),
        in_specs=[IN_VMEM] * (2 + len(greens)),
        out_specs=IN_VMEM,
        out_shape=jax.ShapeDtypeStruct((2 * count, vectors), jnp.float32),
        compiler_params=kernel_params(),
        cost_estimate=NO_COST,
        name="bias_rows",
    )(cholesky, noise, *greens)


def potential_kernel(groups, relative, parts, pieces, *refs):
    sums, chols, refs = refs[:parts], refs[parts : parts + pieces], refs[parts + pieces :]
    before_ref, outs, log_ref = refs[0], refs[2:-1], refs[-1]
    places = [(place, out_ref, j) for group, out_ref in zip(groups, outs) for j, place in enumerate(group)]
    places = [slot for slot in places if slot[0] is not None]
    count = len(places)
    vectors, tile_rows, _ = chols[0].shape
    totals = [ref[...] for ref in sums]
    total = totals[0] + sum(totals[2:], totals[1])
    shifted, log_terms = shifted_field(total[:count, :], total[count:, :])
    own = iota(log_terms.shape, 0) == own_place()
    known = log_ref.shape[0] - 1
    for i in range(known):
        log_ref[i] = before_ref[i]
    log_ref[known] = jnp.sum(jnp.where(own, log_terms, 0.0))
    field = shifted.astype(jnp.bfloat16)
    if relative:
        order = jnp.bitwise_xor(iota((count, count), 0), own_place()) == iota((count, count), 1)
        field = jnp.dot(order.astype(jnp.bfloat16), field, preferred_element_type=jnp.float32).astype(jnp.bfloat16)
    widen = (iota((vectors, vectors * ROWS), 1) // ROWS == iota((vectors, vectors * ROWS), 0)).astype(jnp.bfloat16)
    wide = jnp.dot(field, widen, preferred_element_type=jnp.float32)
    shape = (count, ROWS, vectors * ROWS)
    spread = jnp.where(iota(shape, 1) == iota(shape, 2) % ROWS, wide[:, None, :], 0.0)
    spread = spread.reshape(count * ROWS, vectors * ROWS).astype(jnp.bfloat16)
    for start in range(0, tile_rows, ROWS):
        column = 0
        for chol_ref in chols:
            width = chol_ref.shape[2]
            tile = chol_ref[:, start : start + ROWS, :].reshape(vectors * ROWS, width)
            rows = jnp.dot(spread, tile, preferred_element_type=jnp.float32).astype(jnp.bfloat16)
            for place, out_ref, j in places:
                out_ref[j, start : start + ROWS, column : column + width] = rows[place * ROWS : (place + 1) * ROWS, :]
            column += width


def potential_rows(sums, cholesky, groups, relative, log_steps, after):
    vectors, tile_rows, _ = cholesky[0].shape
    orbitals = sum(piece.shape[2] for piece in cholesky)
    count = sums[0].shape[0] // 2
    known = 0 if log_steps is None else log_steps.shape[0]
    before = jnp.zeros((1,), jnp.float32) if log_steps is None else log_steps
    *blocks, log_steps = pl.pallas_call(
        functools.partial(potential_kernel, groups, relative, len(sums), len(cholesky)),
        in_specs=[IN_VMEM] * (len(sums) + len(cholesky)) + [IN_SMEM, IN_ANY],
        out_specs=[IN_VMEM] * len(groups) + [IN_SMEM],
        out_shape=[
            *(jax.ShapeDtypeStruct((len(group), tile_rows, orbitals), jnp.bfloat16) for group in groups),
            jax.ShapeDtypeStruct((known + 1,), jnp.float32),
        ],
        compiler_params=kernel_params(),
        cost_estimate=NO_COST,
        name="potential_rows",
    )(*sums, *cholesky, before, after)
    return blocks, log_steps


def taylor_steps(potential, term, product_of):
    running = term.astype(jnp.float32)
    for degree in range(1, DEGREES + 1):
        product = (-STEP_ROOT / degree) * product_of(potential, term)
        running = running + product
        term = product.astype(jnp.bfloat16)
    return running.astype(jnp.bfloat16)


def taylor_kernel(k, where, *refs):
    blocks, (walker_ref, _, _, out_ref, held, terms, running, result, written) = refs[:-9], refs[-9:]
    for place, (i, j) in enumerate(where):
        held[device_at(place, True)] = blocks[i][j]
    count, tile_rows, orbitals = held.shape

    def product(degree, term, tiles):
        rows = held[tiles].reshape(-1, orbitals)
        return (-STEP_ROOT / degree) * lax.dot_general(
            term, rows, (((1,), (1,)), ((), ())), preferred_element_type=jnp.float32
        )

    source = walker_ref
    for degree in range(1, DEGREES):
        grown = product(degree, source[...], slice(None))
        source = terms.at[degree % 2]
        source[...] = grown.astype(jnp.bfloat16)
        running[...] = grown + (walker_ref[...].astype(jnp.float32) if degree == 1 else running[...])
    step = max(count // 4, 1)
    writes = []
    for i in range(count // step):
        rows = pl.ds(i * step * tile_rows, step * tile_rows)
        grown = running[:, rows] + product(DEGREES, source[...], slice(i * step, (i + 1) * step))
        result[rows, :] = grown.T.astype(jnp.bfloat16)
        writes.append(pltpu.make_async_copy(result.at[rows], out_ref.at[k, rows], written.at[i]))
        writes[-1].start()
    for write in writes:
        write.wait()


def taylor(blocks, where, walker, k, new, after):
    electrons, orbitals = walker.shape
    count, tile_rows = len(where), blocks[0].shape[1]
    return pl.pallas_call(
        functools.partial(taylor_kernel, k, where),
        in_specs=[IN_VMEM] * (len(blocks) + 1) + [IN_HBM, IN_ANY],
        out_specs=IN_HBM,
        out_shape=jax.ShapeDtypeStruct(new.shape, jnp.bfloat16),
        scratch_shapes=[
            pltpu.VMEM((count, tile_rows, orbitals), jnp.bfloat16),
            pltpu.VMEM((2, electrons, orbitals), jnp.bfloat16),
            pltpu.VMEM((electrons, orbitals), jnp.float32),
            pltpu.VMEM((orbitals, electrons), jnp.bfloat16),
            pltpu.SemaphoreType.DMA((count,)),
        ],
        input_output_aliases={len(blocks) + 1: 0} if k else {},
        compiler_params=kernel_params(),
        cost_estimate=NO_COST,
        name="taylor",
    )(*(in_vmem(block) for block in blocks), walker, in_hbm(new), after)


def swap(block, place):
    if place == 0:
        return block
    planes = lax.axis_size(PLANE)
    return lax.ppermute(block, PLANE, [(i, i ^ place) for i in range(planes)])


def plus_kernel(a_ref, b_ref, *refs):
    refs[-1][...] = a_ref[...] + b_ref[...]


def plus(a, b, after):
    return pl.pallas_call(
        plus_kernel,
        in_specs=[IN_VMEM, IN_VMEM] + [IN_ANY] * len(after),
        out_specs=IN_VMEM,
        out_shape=jax.ShapeDtypeStruct(a.shape, a.dtype),
        compiler_params=kernel_params(),
        cost_estimate=NO_COST,
        name="plus",
    )(a, b, *after)


def join_kernel(moves, sources, *refs):
    outs, arrived = refs[-1 - (len(refs) - sources - 1) // 2 : -1], refs[-1]
    copies = [
        pltpu.make_async_copy(refs[i].at[pl.ds(j, 1)], outs[o].at[pl.ds(q, 1)], arrived.at[m])
        for m, ((i, j), (o, q)) in enumerate(moves)
    ]
    for copy in copies:
        copy.start()
    for copy in copies:
        copy.wait()


def join(sources, targets, moves):
    return pl.pallas_call(
        functools.partial(join_kernel, moves, len(sources)),
        in_specs=[IN_ANY] * (len(sources) + len(targets)),
        out_specs=[IN_ANY] * len(targets),
        out_shape=[jax.ShapeDtypeStruct(target.shape, target.dtype) for target in targets],
        input_output_aliases={len(sources) + i: i for i in range(len(targets))},
        scratch_shapes=[pltpu.SemaphoreType.DMA((len(moves),))],
        compiler_params=kernel_params(),
        cost_estimate=NO_COST,
        name="join",
    )(*sources, *targets)


def staged_groups(along_wa, along_col):
    return (
        (0,),
        *(tuple(range(a * along_col, (a + 1) * along_col)) for a in range(1, along_wa)),
        *((c, *(None,) * (along_wa - 1)) for c in range(1, along_col)),
    )


def stage_along_wa(blocks, along_wa, along_col):
    passed = {a: swap(blocks[a], a * along_col) for a in reversed(range(1, along_wa))}
    return [passed[a] for a in range(1, along_wa)]


def stage_along_col(blocks, first, along_wa, along_col, after):
    second = blocks[along_wa:]
    if first and second:
        moves = tuple(((along_wa - 1 - a, c), (c - 1, a)) for a in range(1, along_wa) for c in range(1, along_col))
        second = join([*reversed(first), *after], second, moves)
    second = [swap(block, c) for c, block in enumerate(second, 1)]
    where = tuple((along_wa + c - 1, a) if c else (a, 0) for a in range(along_wa) for c in range(along_col))
    return [blocks[0], *first, *second], where


def by_permutes(walkers, intersection_inverse, noise_index, cholesky):
    walker_count = walkers.shape[0]
    tile_rows = cholesky.shape[1]
    planes = lax.axis_size(PLANE)
    along_wa, along_col = lax.axis_size("wa"), lax.axis_size("col")
    half, half_wa = planes // 2, along_wa // 2
    far, near = tuple(range(half, planes)), tuple(range(half))
    noise = quantile(noise_index)
    direct = tuple((p,) for p in range(planes))
    staged = staged_groups(along_wa, along_col)

    def make_green(k, groups, after):
        return green_rows(walkers, intersection_inverse, k, tile_rows, groups, True, after)

    def ordered(received):
        places = (*far[:1], *near[along_col:], *far[1:], *near[:along_col])
        return [received[p] for p in places], tuple((places.index(p), 0) for p in range(planes))

    short = along_wa - 1
    staged_short = staged_groups(short, along_col)
    last_ones = tuple((p,) for p in range(short * along_col, planes))
    one = make_green(0, staged_short[1:short], walkers)
    two = make_green(0, (*last_ones, staged_short[0], *staged_short[short:]), one[0])
    blocks = [two[along_col], *one, *two[along_col + 1 :]]
    orbitals, electrons = walkers.shape[1:]
    cut = orbitals // 2 if orbitals % 512 == 0 and electrons <= orbitals // 2 else orbitals
    held = [load(cholesky, 0, cut, two[0])]
    rest = [(cut, cut + (orbitals - cut) // 2), (cut + (orbitals - cut) // 2, orbitals)] if cut < orbitals else []
    direct_ones = [swap(block, p) for (p,), block in zip(last_ones, two)]
    passing = stage_along_wa(blocks, short, along_col)
    staged_ones, where = stage_along_col(blocks, passing, short, along_col, held)
    greens = (
        [*direct_ones, *staged_ones],
        (*((i + along_col, j) for i, j in where), *((i, 0) for i in range(along_col))),
        True,
    )
    token = passing[-1]

    def reduced(sums, wanted):
        distance = 1
        while distance < half:
            if rest:
                held.append(load(cholesky, *rest.pop(0), sums))
            if 2 * distance == half:
                brought.update({i: bring(walkers, i, sums) for i in wanted})
            sums = plus(sums, swap(sums, distance), [held[-1], *brought.values()])
            distance *= 2
        sums = [sums]
        for j in range(half_wa):
            pairs = ((0, half_wa + j), (along_wa - 1, half_wa - 1 - j))
            sums.append(lax.ppermute(sums[0], "wa", pairs))
        return sums

    new, log_steps, brought = walkers, None, {}
    waiting = None
    for k in range(walker_count):
        last = k == walker_count - 1
        if not last:
            later = make_green(k + 1, staged, token)
            token = later[0]
            coming = stage_along_wa(later, along_wa, along_col)
        sums = bias_rows(held[0], noise[k : k + 1], *greens)
        wanted = [i for i in (k - 1, k) if 0 <= i and (i < k or last)]
        parts = reduced(sums, wanted)
        if waiting is not None:
            first = stage_along_wa(waiting, along_wa, along_col)
        groups = direct if last else staged
        after = sums if last else coming[half_wa - 1]
        blocks, log_steps = potential_rows(parts, held, groups, True, log_steps, after)
        got = {p: swap(blocks[p], p) for p in (*far[:1], *near[along_col:], *far[1:], *near[:along_col])} if last else {}
        if waiting is not None:
            passed = [blocks[0]]
            new = taylor(*stage_along_col(waiting, first, along_wa, along_col, passed), brought.pop(k - 1), k - 1, new, walkers)
        if last:
            new = taylor(*ordered(got), brought[k], k, new, walkers)
        else:
            waiting = blocks
            greens = (*stage_along_col(later, coming, along_wa, along_col, [log_steps]), True)
    return new, log_steps


def by_all_to_all(walkers, intersection_inverse, noise_index, cholesky):
    walker_count, orbitals, electrons = walkers.shape
    vectors, tile_rows, _ = cholesky.shape
    planes = lax.axis_size(PLANE)
    green = jnp.einsum(
        "kpe,kef->kpf", walkers, intersection_inverse, preferred_element_type=jnp.float32
    ).astype(jnp.bfloat16)
    green = lax.all_to_all(
        green.reshape(walker_count, planes, tile_rows, electrons), PLANE, split_axis=1, concat_axis=1, tiled=True
    )
    partial_sums = jnp.einsum(
        "kspe,gpe->ksg", green, cholesky[:, :, :electrons], preferred_element_type=jnp.float32
    )
    bias_sum = lax.psum(partial_sums, PLANE)
    noise = lax.all_gather(quantile(noise_index), PLANE, axis=1, tiled=False)
    shifted, log_terms = shifted_field(bias_sum, noise)
    log_weight = lax.dynamic_index_in_dim(jnp.sum(log_terms, axis=-1), lax.axis_index(PLANE), 1, keepdims=False)
    rows = jnp.einsum(
        "ksg,gpq->kspq", shifted.astype(jnp.bfloat16), cholesky, preferred_element_type=jnp.float32
    ).astype(jnp.bfloat16)
    potential = lax.all_to_all(rows, PLANE, split_axis=1, concat_axis=1, tiled=True)
    new = taylor_steps(
        potential.reshape(walker_count, orbitals, orbitals),
        walkers,
        lambda a, b: jnp.einsum("kpq,kqe->kpe", a, b, preferred_element_type=jnp.float32),
    )
    return new, log_weight


def per_device(walkers, intersection_inverse, noise_index, cholesky):
    planes = lax.axis_size(PLANE)
    tile_rows = cholesky.shape[1]
    permutes = (
        4 <= lax.axis_size("wa")
        and planes <= MOST_PERMUTES
        and planes & (planes - 1) == 0
        and tile_rows % ROWS == 0
    )
    step = by_permutes if permutes else by_all_to_all
    return step(walkers, intersection_inverse, noise_index, cholesky)


def solution(mesh):
    placed = (
        P(("grp", "wa", "col", "row"), None, None),
        P(("grp", "wa", "col", "row"), None, None),
        P(("grp", "wa", "col", "row"), None),
        P(None, ("wa", "col"), None),
    )
    return jax.shard_map(
        per_device,
        mesh=mesh,
        in_specs=placed,
        out_specs=(P(("grp", "wa", "col", "row"), None, None), P(("grp", "wa", "col", "row"))),
        check_vma=False,
    )
```
